32 devices in a mesh: dp: 4 (over y, x), ctx: 8 (over z, core).
Axes of the slice: x: 2, y: 2, z: 4, core: 2. Of those that a mesh axis runs over, the one named last changes fastest.
Arguments:
- queries: bfloat16 [4, 1024, 1024], P('dp', 'ctx'), may hold values from -180 to 180
- keys: bfloat16 [4, 4096, 128], P('dp', 'ctx'), may hold values from -6 to 6
- values: bfloat16 [4, 4096, 128], P('dp', 'ctx'), may hold values from -6 to 6
- grad_out: bfloat16 [4, 1024, 1024], P('dp', 'ctx'), may hold values from -6 to 6
- saved_out: bfloat16 [4, 1024, 1024], P('dp', 'ctx'), may hold values from -1.796875 to 1.796875
- segment_ids: int32 [4, 4096], P('dp', 'ctx'), may hold values from 0 to 31, never falling along the last dimension, each value on 1 to 1024 neighbouring positions
- frame_flags: int32 [4, 32], P('dp'), may hold values 0 or 1
Outputs:
- grad_queries: bfloat16 [4, 1024, 1024], P('dp', 'ctx')
- grad_keys: bfloat16 [4, 4096, 128], P('dp', 'ctx')
- grad_values: bfloat16 [4, 4096, 128], P('dp', 'ctx')
The draws below stay inside these ranges and needn't reach their ends.
All inputs are finite; a program needn't handle non-finite values. No bound on the sum of `frame_flags` on one device may be relied on, other than what follows from the above.
Results may differ from the reference program's by a relative error of at most 0.0051.
Values may be sent and summed in bfloat16 or wider, within the bound.
A program may use at most 64 MiB of HBM per device.

```python
import math
import jax
import jax.numpy as jnp
import numpy as np
from jax import lax

H = 8
HD = 128
KEY_DEV = 512
Q_DEV = 128
SEQS = 4
SEQ_LEN = 4096
QROWS = 1024
NSEG = 32
SEG_MOST = 1024
N_CTX = 8


def paired_draw(key):
    query_seed = jax.random.fold_in(key, 101)
    key_seed = jax.random.fold_in(key, 202)
    key_field = jnp.clip(jax.random.normal(key_seed, (SEQS, SEQ_LEN, HD), jnp.float32), -6.0, 6.0)
    query_field = jnp.clip(jax.random.normal(query_seed, (SEQS, QROWS, H * HD), jnp.float32), -6.0, 6.0)
    return (query_field, key_field)


def draw_queries(key, part):
    return paired_draw(key)[0].astype(jnp.bfloat16)


def draw_keys(key, part):
    return paired_draw(key)[1].astype(jnp.bfloat16)


def with_ends(values, key, low, top_value):
    dims = values.shape
    place = [jax.random.randint(jax.random.fold_in(key, axis), (), 0, dims[axis]) for axis in range(len(dims))]
    values = values.at[tuple(place)].set(low)
    longest = dims.index(max(dims))
    place[longest] = (place[longest] + 1) % dims[longest]
    return values.at[tuple(place)].set(top_value)


def levels(own_key, extent, pieces, low, largest):
    def one(position, parts):
        heights = jax.random.uniform(jax.random.fold_in(jax.random.fold_in(own_key, 6), position), (parts,), jnp.float32, low / len(pieces), largest / len(pieces))
        return jnp.repeat(jnp.exp(heights), extent[position] // parts).reshape((-1,) + (1,) * (len(extent) - position - 1))

    loudness = one(*pieces[0])
    for cut in pieces[1:]:
        loudness = loudness * one(*cut)
    return loudness


def split_up(count, total, reach, lean):
    loads = [(1 << 20) // math.isqrt(grade ** lean) + 1 for grade in range(2, count + 1)]
    spare, holding = total - reach - (count - 1), [1] * (count - 1)
    while spare > 0:
        candidates = [i for i in range(count - 1) if holding[i] < reach]
        whole, left = sum([loads[i] for i in candidates]), spare
        for i in candidates:
            addition = min(reach - holding[i], max(1, left * loads[i] // whole), spare)
            holding[i] = holding[i] + addition
            spare = spare - addition
    return np.array([reach] + holding)


def uneven_parts(rng, amount, total, reach, skew):
    if amount == 2:
        one = jax.random.randint(rng, (), max(1, total - reach), min(reach, total - 1) + 1)
        return jnp.stack([one, total - one])
    lengths = jnp.asarray(split_up(amount, total, reach, skew), jnp.int32)
    twos = (amount - 1) // 2
    source_of, receiver = lengths[1:1 + 2 * twos:2], lengths[2:2 + 2 * twos:2]
    room = jnp.minimum(source_of - 1, reach - receiver)
    shifted = jax.random.randint(jax.random.fold_in(rng, 1), (twos,), 0, 1 << 20) % (room + 1)
    lengths = lengths.at[1:1 + 2 * twos:2].set(source_of - shifted).at[2:2 + 2 * twos:2].set(receiver + shifted)
    return lengths[jax.random.permutation(jax.random.fold_in(rng, 2), amount)]


def bell_draw(own_key, dims, scale, most, pieces=(), kind=jnp.bfloat16):
    loudness = levels(own_key, dims, pieces, -0.22, 0.18) if pieces else 1.0
    values = jax.random.normal(own_key, dims, jnp.float32) * scale * loudness
    return jnp.minimum(jnp.maximum(values, -most), most).astype(kind)


def setup_inputs(seed: int = 0) -> dict:
    arg_keys = jax.random.split(jax.random.key(seed), 8)
    queries = draw_queries(jax.random.fold_in(arg_keys[7], 71), 0)
    keys = draw_keys(jax.random.fold_in(arg_keys[7], 71), 0)
    values = bell_draw(arg_keys[2], (SEQS, SEQ_LEN, HD), 1.0, 6.0, ((0, 4), (1, 8)))
    grad_out = bell_draw(arg_keys[3], (SEQS, QROWS, H * HD), 1.0, 6.0, ((0, 4), (1, 8)))
    saved_out = bell_draw(arg_keys[4], (SEQS, QROWS, H * HD), 0.3, 1.796875, ((0, 4), (1, 8)))
    segment_ids = jax.vmap(lambda own: jnp.searchsorted(jnp.cumsum(uneven_parts(own, NSEG, SEQ_LEN, SEG_MOST, 2)), jnp.arange(SEQ_LEN), side="right"))(jax.random.split(arg_keys[5], SEQS)).reshape((SEQS, SEQ_LEN)).astype(jnp.int32)
    frame_flags = with_ends((jax.random.randint(arg_keys[6], (SEQS, NSEG), 0, 2) < 1).astype(jnp.int32), jax.random.fold_in(arg_keys[6], 1), 0, 1)
    return {"queries": queries, "keys": keys, "values": values, "grad_out": grad_out, "saved_out": saved_out, "segment_ids": segment_ids, "frame_flags": frame_flags}


def reference(queries, keys, values, grad_out, saved_out, segment_ids, frame_flags):
    score_scale = 1.0 / math.sqrt(HD)
    segment_count = frame_flags.shape[1]

    def one_sequence(operands):
        query_seq, key_seq, value_seq, grad_seq, saved_seq, seg_seq, flag_seq = operands
        onehot = seg_seq[:, None] == jnp.arange(segment_count, dtype=jnp.int32)[None, :]
        frame_of = lax.optimization_barrier(jnp.sum(jnp.where(onehot, flag_seq[None, :], 0), axis=1))
        key_pos = jnp.arange(SEQ_LEN, dtype=jnp.int32)

        def window(carried, rank_index):
            key_grad, value_grad = carried
            row_first = (rank_index * Q_DEV).astype(jnp.int32)
            pos_first = (rank_index * KEY_DEV + KEY_DEV - Q_DEV).astype(jnp.int32)
            query_mat = lax.dynamic_slice_in_dim(query_seq, row_first, Q_DEV, 0).reshape(Q_DEV * H, HD)
            grad_mat = lax.dynamic_slice_in_dim(grad_seq, row_first, Q_DEV, 0)
            saved_mat = lax.dynamic_slice_in_dim(saved_seq, row_first, Q_DEV, 0)
            out_dot = lax.optimization_barrier(jnp.sum((grad_mat.astype(jnp.float32) * saved_mat.astype(jnp.float32)).reshape(Q_DEV * H, HD), axis=1))
            grad_mat = grad_mat.reshape(Q_DEV * H, HD)
            query_pos = pos_first + jnp.arange(Q_DEV, dtype=jnp.int32)
            query_seg = lax.dynamic_slice_in_dim(seg_seq, pos_first, Q_DEV)
            query_frame = lax.dynamic_slice_in_dim(frame_of, pos_first, Q_DEV)
            row_pos = jnp.repeat(query_pos, H)
            row_seg = jnp.repeat(query_seg, H)
            row_frame = jnp.repeat(query_frame, H) == 1
            visible = (key_pos[None, :] <= row_pos[:, None]) | (seg_seq[None, :] == row_seg[:, None]) & row_frame[:, None]
            scores = jnp.dot(query_mat, key_seq.T, preferred_element_type=jnp.float32) * score_scale
            row_top = lax.optimization_barrier(jnp.max(jnp.where(visible, scores, -jnp.inf), axis=1))
            log_total = row_top + jnp.log(lax.optimization_barrier(jnp.sum(jnp.where(visible, jnp.exp(scores - row_top[:, None]), 0.0), axis=1)))
            probs = jnp.where(visible, jnp.exp(scores - log_total[:, None]), 0.0)
            probs_low = probs.astype(jnp.bfloat16)
            dprobs = jnp.dot(grad_mat, value_seq.T, preferred_element_type=jnp.float32)
            dscores = (probs * (dprobs - out_dot[:, None])).astype(jnp.bfloat16)
            query_grad = (score_scale * jnp.dot(dscores, key_seq, preferred_element_type=jnp.float32)).astype(jnp.bfloat16)
            key_grad = key_grad + score_scale * jnp.dot(dscores.T, query_mat, preferred_element_type=jnp.float32)
            value_grad = value_grad + jnp.dot(probs_low.T, grad_mat, preferred_element_type=jnp.float32)
            return ((key_grad, value_grad), query_grad.reshape(Q_DEV, H * HD))
        initial = (jnp.zeros((SEQ_LEN, HD), jnp.float32), jnp.zeros((SEQ_LEN, HD), jnp.float32))
        (key_grad, value_grad), query_grads = lax.scan(window, initial, jnp.arange(N_CTX, dtype=jnp.int32))
        return (query_grads.reshape(QROWS, H * HD), key_grad.astype(jnp.bfloat16), value_grad.astype(jnp.bfloat16))
    grad_queries, grad_keys, grad_values = lax.map(one_sequence, (queries, keys, values, grad_out, saved_out, segment_ids, frame_flags))
    return (grad_queries, grad_keys, grad_values)
```

```python
import functools
import math

import jax
import jax.numpy as jnp
from jax import lax
from jax.experimental import pallas as pl
from jax.experimental.pallas import tpu as pltpu
from jax.sharding import PartitionSpec as P

HD = 128
SEG_MOST = 1024
CORES = 2
LOW = -1e30
FLOOR = -1e29
KEEP_BYTES = 20 * 1024 * 1024
F32 = jnp.float32
BF16 = jnp.bfloat16


def push(src, dst, send, recv, rank):
    return pltpu.make_async_remote_copy(
        src_ref=src,
        dst_ref=dst,
        send_sem=send,
        recv_sem=recv,
        device_id={"ctx": rank},
        device_id_type=pl.DeviceIdType.MESH,
    )


def fused(
    ranks, look, chunk, keep,
    q_ref, k_ref, v_ref, do_ref, o_ref, seg_ref, flag_ref,
    dq_ref, dk_ref, dv_ref,
    kbuf, vbuf, ebuf, tops, qcols, qrows, docols, dorows, reach, odot, top, total, lse, dqt,
    gpart, sib_out, sib_in, ch_out, ch_in, low_in, segs,
    k_up, k_side, k_down, k_recv, v_up, v_side, v_down, v_recv,
    gs_send, gs_recv, gc_send, gc_recv, gl_send, gl_recv, seg_send, seg_recv,
):
    chips = ranks // CORES
    key_rows = k_ref.shape[0]
    query_rows = q_ref.shape[0]
    heads = q_ref.shape[1] // HD
    cols = query_rows * heads
    parts = key_rows // chunk
    scale = 1.0 / math.sqrt(HD)
    factor = scale * math.log2(math.e)
    me = lax.axis_index("ctx")
    chip = me // CORES
    core = me % CORES
    side = chip * CORES + (1 - core)
    is_top = chip == chips - 1
    not_top = chip < chips - 1
    has_low = chip > 0
    own_slot = me
    reach_ranks = max(look, CORES)

    barrier = pltpu.get_barrier_semaphore()
    there = jnp.int32(0)
    for d in range(1, reach_ranks + 1):
        @pl.when(me + d < ranks)
        def _():
            pl.semaphore_signal(barrier, inc=1, device_id={"ctx": me + d},
                                device_id_type=pl.DeviceIdType.MESH)

        @pl.when(me - d >= 0)
        def _():
            pl.semaphore_signal(barrier, inc=1, device_id={"ctx": me - d},
                                device_id_type=pl.DeviceIdType.MESH)

        there = there + jnp.where(me + d < ranks, 1, 0) + jnp.where(me - d >= 0, 1, 0)
    kbuf[own_slot] = k_ref[...]
    vbuf[own_slot] = v_ref[...]
    pl.semaphore_wait(barrier, there)

    def up(buf, sems, recv, w):
        slot = w * CORES + core
        return push(buf.at[slot], buf.at[slot], sems.at[w], recv.at[slot], me + CORES)

    def across(buf, sems, recv, w):
        slot = w * CORES + core
        return push(buf.at[slot], buf.at[slot], sems.at[w], recv.at[slot], side)

    def down(buf, sems, recv):
        return push(buf.at[own_slot], buf.at[own_slot], sems.at[0], recv.at[own_slot], me - CORES)

    def arrived(buf, sems, recv, slot):
        push(buf.at[slot], buf.at[slot], sems.at[0], recv.at[slot], side).wait_recv()

    def seg_copy(d, rank):
        return push(seg_ref, segs.at[d - 1], seg_send.at[d - 1], seg_recv.at[d - 1], rank)

    def grad_side(kind, w):
        return push(sib_out.at[kind, w], sib_in.at[kind, w], gs_send.at[kind, w], gs_recv.at[kind, w], side)

    def grad_down(kind, w):
        return push(ch_out.at[kind, w], ch_in.at[kind, w], gc_send.at[kind, w], gc_recv.at[kind, w], me - CORES)

    def grad_up(kind):
        return push(ch_out.at[kind, chip + 1], low_in.at[kind], gl_send.at[kind], gl_recv.at[kind], me + CORES)

    @pl.when(not_top)
    def _():
        up(kbuf, k_up, k_recv, chip).start()

    across(kbuf, k_side, k_recv, chip).start()
    for d in range(1, look + 1):
        @pl.when(me - d >= 0)
        def _():
            seg_copy(d, me - d).start()

    @pl.when(has_low)
    def _():
        down(kbuf, k_down, k_recv).start()
        down(vbuf, v_down, v_recv).start()

    across(vbuf, v_side, v_recv, chip).start()

    for h in range(heads):
        at = slice(h * HD, (h + 1) * HD)
        rows = slice(h * query_rows, (h + 1) * query_rows)
        q_h = q_ref[:, at]
        do_h = do_ref[:, at]
        qrows[rows, :] = q_h
        dorows[rows, :] = do_h
        qcols[:, rows] = q_h.T
        docols[:, rows] = do_h.T
        odot[:, rows] = jnp.sum((do_h.astype(F32) * o_ref[:, at].astype(F32)).T, axis=0, keepdims=True)
    top[...] = jnp.full(top.shape, FLOOR, F32)
    total[...] = jnp.zeros(total.shape, F32)
    dqt[...] = jnp.zeros(dqt.shape, F32)

    for d in range(1, look + 1):
        @pl.when(me + d < ranks)
        def _():
            seg_copy(d, side).wait_recv()

        @pl.when(me + d >= ranks)
        def _():
            segs[d - 1] = jnp.full(seg_ref.shape, 1 << 20, jnp.int32)

    seg_q = seg_ref[:, key_rows - query_rows:].astype(F32)
    seg_col = jnp.broadcast_to(seg_q, (HD, query_rows)).T
    counts = jnp.zeros((query_rows, HD), F32)
    for d in range(look + 1):
        for j in range(key_rows // HD):
            at = slice(j * HD, (j + 1) * HD)
            piece = (seg_ref[:, at] if d == 0 else segs[d - 1, :, at]).astype(F32)
            counts = counts + jnp.where(piece <= seg_col, 1.0, 0.0)
    count = jnp.sum(counts, axis=1, keepdims=True)
    segments = flag_ref.shape[1]
    ids = lax.broadcasted_iota(jnp.int32, (query_rows, segments), 1).astype(F32)
    flags = jnp.broadcast_to(flag_ref[...].astype(F32), (query_rows, segments))
    framed = jnp.sum(jnp.where(ids == seg_col[:, :1], flags, 0.0), axis=1, keepdims=True)
    local = (key_rows - query_rows) + lax.broadcasted_iota(jnp.int32, (query_rows, 1), 0).astype(F32)
    last = jnp.where(framed == 1.0, count - 1.0, local)
    last_row = jnp.broadcast_to(last, (query_rows, HD)).T[:1, :].astype(jnp.int32) + me * key_rows
    for h in range(heads):
        reach[:, h * query_rows:(h + 1) * query_rows] = last_row

    def rows_of(part):
        return pl.ds(pl.multiple_of(part * chunk, chunk), chunk)

    def scores_of(slot, part, masked):
        s = jnp.dot(kbuf[slot, rows_of(part), :], qcols[...], preferred_element_type=F32) * factor
        if masked:
            first = slot * key_rows + part * chunk
            pos = first + lax.broadcasted_iota(jnp.int32, (chunk, cols), 0)
            s = jnp.where(pos <= reach[...], s, LOW)
        return s

    def stats(slot, masked):
        @pl.loop(0, parts)
        def _(part):
            s = scores_of(slot, part, masked)
            here = jnp.maximum(jnp.max(s, axis=0, keepdims=True), FLOOR)
            e = jnp.exp2(s - here)
            if keep:
                ebuf[slot, rows_of(part), :] = e
                tops[slot * parts + part] = here
            old = top[...]
            new = jnp.maximum(old, here)
            total[...] = total[...] * jnp.exp2(old - new) + (
                jnp.sum(e, axis=0, keepdims=True) * jnp.exp2(here - new))
            top[...] = new

    def chip_stats(w, masked):
        @pl.loop(0, CORES)
        def _(b):
            slot = w * CORES + (core + b) % CORES

            @pl.when(b == 1)
            def _():
                arrived(kbuf, k_side, k_recv, slot)

            stats(slot, masked)

    def probs_of(slot, part, masked):
        if keep:
            return ebuf[slot, rows_of(part), :] * jnp.exp2(tops[slot * parts + part] - lse[...])
        return jnp.exp2(scores_of(slot, part, masked) - lse[...])

    def send_side(kind, w):
        sib_out[kind, w] = gpart[kind, w * CORES + (1 - core)].astype(BF16)
        grad_side(kind, w).start()

    def value_grads(w, masked):
        @pl.loop(0, CORES * parts)
        def _(i):
            slot = w * CORES + i // parts
            part = i % parts
            p = probs_of(slot, part, masked).astype(BF16)
            gpart[0, slot, rows_of(part), :] = jnp.dot(p, dorows[...], preferred_element_type=F32)

        send_side(0, w)

    def key_grads(w, masked):
        @pl.loop(0, CORES)
        def _(b):
            slot = w * CORES + (core + b) % CORES

            @pl.when(b == 1)
            def _():
                arrived(vbuf, v_side, v_recv, slot)

            @pl.loop(0, parts)
            def _(part):
                p = probs_of(slot, part, masked)
                dp = jnp.dot(vbuf[slot, rows_of(part), :], docols[...], preferred_element_type=F32)
                ds = (p * (dp - odot[...])).astype(BF16)
                gpart[1, slot, rows_of(part), :] = scale * jnp.dot(ds, qrows[...], preferred_element_type=F32)
                dqt[...] += jnp.dot(kbuf[slot, rows_of(part), :].T, ds, preferred_element_type=F32)

        send_side(1, w)

    def summed(kind, w):
        grad_side(kind, w).wait_recv()
        return gpart[kind, w * CORES + core] + sib_in[kind, w].astype(F32)

    def hand_down(kind, w):
        ch_out[kind, w] = summed(kind, w).astype(BF16)

        @pl.when(not_top)
        def _():
            grad_down(kind, w).wait_recv()
            ch_out[kind, w] = (summed_again(kind, w) + ch_in[kind, w].astype(F32)).astype(BF16)

        grad_down(kind, w).start()

    def summed_again(kind, w):
        return gpart[kind, w * CORES + core] + sib_in[kind, w].astype(F32)

    @pl.when(jnp.logical_and(not_top, chip == 0))
    def _():
        up(vbuf, v_up, v_recv, chip).start()

    chip_stats(chip, True)

    @pl.loop(1, chip + 1)
    def _(s):
        w = chip - s
        arrived(kbuf, k_side, k_recv, w * CORES + core)

        @pl.when(not_top)
        def _():
            up(kbuf, k_up, k_recv, w).start()

        across(kbuf, k_side, k_recv, w).start()

        @pl.when(jnp.logical_and(not_top, w == 0))
        def _():
            up(vbuf, v_up, v_recv, chip).start()

        chip_stats(w, False)

    @pl.when(not_top)
    def _():
        arrived(kbuf, k_side, k_recv, (chip + 1) * CORES + core)
        across(kbuf, k_side, k_recv, chip + 1).start()
        chip_stats(chip + 1, True)

    lse[...] = top[...] + jnp.log(total[...]) * math.log2(math.e)

    @pl.loop(0, chip)
    def _(t):
        w = chip - 1 - t
        value_grads(w, False)

        @pl.when(not_top)
        def _():
            arrived(vbuf, v_side, v_recv, w * CORES + core)
            up(vbuf, v_up, v_recv, w).start()
            across(vbuf, v_side, v_recv, w).start()

        @pl.when(jnp.logical_and(is_top, t > 0))
        def _():
            hand_down(0, w + 1)

    @pl.when(jnp.logical_and(is_top, has_low))
    def _():
        hand_down(0, 0)

    @pl.loop(0, chip)
    def _(t):
        w = chip - 1 - t

        @pl.when(is_top)
        def _():
            arrived(vbuf, v_side, v_recv, w * CORES + core)
            across(vbuf, v_side, v_recv, w).start()

        key_grads(w, False)

        @pl.when(jnp.logical_and(is_top, t > 0))
        def _():
            hand_down(1, w + 1)

        @pl.when(not_top)
        def _():
            hand_down(0, w)

    @pl.when(jnp.logical_and(is_top, has_low))
    def _():
        hand_down(1, 0)

    end = jnp.where(not_top, 2, 1)

    @pl.loop(0, end)
    def _(t):
        w = chip + end - 1 - t
        value_grads(w, True)

        @pl.when(w > chip)
        def _():
            arrived(vbuf, v_side, v_recv, w * CORES + core)
            across(vbuf, v_side, v_recv, w).start()

        key_grads(w, True)

        @pl.when(w > chip)
        def _():
            for kind in range(2):
                ch_out[kind, w] = summed(kind, w).astype(BF16)
                grad_up(kind).start()

    @pl.when(not_top)
    def _():
        @pl.loop(0, chip)
        def _(t):
            hand_down(1, chip - 1 - t)

    for h in range(heads):
        rows = slice(h * query_rows, (h + 1) * query_rows)
        dq_ref[:, h * HD:(h + 1) * HD] = (dqt[:, rows].T * scale).astype(BF16)

    for kind, out in ((0, dv_ref), (1, dk_ref)):
        gpart[kind, own_slot] = summed(kind, chip)

        @pl.when(has_low)
        def _():
            push(low_in.at[kind], low_in.at[kind], gl_send.at[kind], gl_recv.at[kind], side).wait_recv()
            gpart[kind, own_slot] = gpart[kind, own_slot] + low_in[kind].astype(F32)

        @pl.when(not_top)
        def _():
            grad_down(kind, chip).wait_recv()
            gpart[kind, own_slot] = gpart[kind, own_slot] + ch_in[kind, chip].astype(F32)

        out[...] = gpart[kind, own_slot].astype(BF16)

    for d in range(1, look + 1):
        @pl.when(me - d >= 0)
        def _():
            seg_copy(d, side).wait_send()

    @pl.when(has_low)
    def _():
        down(kbuf, k_down, k_recv).wait_send()
        down(vbuf, v_down, v_recv).wait_send()

    @pl.when(not_top)
    def _():
        for kind in range(2):
            grad_up(kind).wait_send()

    @pl.loop(0, chip + end)
    def _(w):
        across(kbuf, k_side, k_recv, w).wait_send()
        across(vbuf, v_side, v_recv, w).wait_send()
        for kind in range(2):
            grad_side(kind, w).wait_send()

        @pl.when(jnp.logical_and(not_top, w <= chip))
        def _():
            up(kbuf, k_up, k_recv, w).wait_send()
            up(vbuf, v_up, v_recv, w).wait_send()

        @pl.when(w < chip)
        def _():
            for kind in range(2):
                grad_down(kind, w).wait_send()


def per_device(queries, keys, values, grad_out, saved_out, segment_ids, frame_flags):
    ranks = lax.axis_size("ctx")
    chips = ranks // CORES
    key_rows = keys.shape[1]
    query_rows, width = queries.shape[1:]
    cols = query_rows * (width // HD)
    look = (SEG_MOST + key_rows - 2) // key_rows
    assert look <= CORES and ranks % CORES == 0
    chunk = math.gcd(key_rows, 256)
    parts = key_rows // chunk
    keep = ranks * key_rows * cols * 4 <= KEEP_BYTES
    kept = ranks if keep else 1
    dma = pltpu.SemaphoreType.DMA
    block = (key_rows, HD)
    grads = (2, chips) + block
    vmem = pl.BlockSpec(memory_space=pltpu.VMEM)
    grad_queries, grad_keys, grad_values = pl.pallas_call(
        functools.partial(fused, ranks, look, chunk, keep),
        out_shape=(
            jax.ShapeDtypeStruct((query_rows, width), BF16),
            jax.ShapeDtypeStruct(block, BF16),
            jax.ShapeDtypeStruct(block, BF16),
        ),
        in_specs=[vmem] * 7,
        out_specs=(vmem,) * 3,
        scratch_shapes=[
            pltpu.VMEM((ranks,) + block, BF16),
            pltpu.VMEM((ranks,) + block, BF16),
            pltpu.VMEM((kept, key_rows, cols), F32) if keep else pltpu.VMEM((8, 128), F32),
            pltpu.VMEM((kept * parts, 1, cols), F32),
            pltpu.VMEM((HD, cols), BF16),
            pltpu.VMEM((cols, HD), BF16),
            pltpu.VMEM((HD, cols), BF16),
            pltpu.VMEM((cols, HD), BF16),
            pltpu.VMEM((1, cols), jnp.int32),
            pltpu.VMEM((1, cols), F32),
            pltpu.VMEM((1, cols), F32),
            pltpu.VMEM((1, cols), F32),
            pltpu.VMEM((1, cols), F32),
            pltpu.VMEM((HD, cols), F32),
            pltpu.VMEM((2, ranks) + block, F32),
            pltpu.VMEM(grads, BF16),
            pltpu.VMEM(grads, BF16),
            pltpu.VMEM(grads, BF16),
            pltpu.VMEM(grads, BF16),
            pltpu.VMEM((2,) + block, BF16),
            pltpu.VMEM((look, 1, key_rows), jnp.int32),
            dma((chips,)), dma((chips,)), dma((1,)), dma((ranks,)),
            dma((chips,)), dma((chips,)), dma((1,)), dma((ranks,)),
            dma((2, chips)), dma((2, chips)), dma((2, chips)), dma((2, chips)),
            dma((2,)), dma((2,)), dma((look,)), dma((look,)),
        ],
        compiler_params=pltpu.CompilerParams(
            collective_id=0, has_side_effects=True, vmem_limit_bytes=60 * 1024 * 1024
        ),
        cost_estimate=pl.CostEstimate(
            flops=12 * cols * ranks * key_rows * HD,
            bytes_accessed=8 * cols * HD,
            transcendentals=cols * ranks * key_rows,
        ),
    )(queries[0], keys[0], values[0], grad_out[0], saved_out[0], segment_ids, frame_flags)
    return grad_queries[None], grad_keys[None], grad_values[None]


def solution(mesh):
    return jax.shard_map(
        per_device,
        mesh=mesh,
        in_specs=(
            P("dp", "ctx", None),
            P("dp", "ctx", None),
            P("dp", "ctx", None),
            P("dp", "ctx", None),
            P("dp", "ctx", None),
            P("dp", "ctx"),
            P("dp", None),
        ),
        out_specs=(P("dp", "ctx", None), P("dp", "ctx", None), P("dp", "ctx", None)),
        check_vma=False,
    )
```

```python
import functools
import math

import jax
import jax.numpy as jnp
from jax import lax
from jax.experimental import pallas as pl
from jax.experimental.pallas import tpu as pltpu
from jax.sharding import PartitionSpec as P

HD = 128
SEG_MOST = 1024
CORES = 2
LOW = -1e30
FLOOR = -1e29
KEEP_BYTES = 20 * 1024 * 1024
F32 = jnp.float32
BF16 = jnp.bfloat16


def push(src, dst, send, recv, rank):
    return pltpu.make_async_remote_copy(
        src_ref=src,
        dst_ref=dst,
        send_sem=send,
        recv_sem=recv,
        device_id={"ctx": rank},
        device_id_type=pl.DeviceIdType.MESH,
    )


def fused(
    ranks, look, chunk, keep,
    q_ref, k_ref, v_ref, do_ref, o_ref, seg_ref, flag_ref,
    dq_ref, dk_ref, dv_ref,
    kbuf, vbuf, ebuf, tops, qcols, qrows, docols, dorows, reach, odot, top, total, lse, dqt,
    gpart, sib_out, sib_in, ch_out, ch_in, low_in, segs,
    k_up, k_side, k_down, k_recv, v_up, v_side, v_down, v_recv,
    gs_send, gs_recv, gc_send, gc_recv, gl_send, gl_recv, seg_send, seg_recv,
):
    chips = ranks // CORES
    key_rows = k_ref.shape[0]
    query_rows = q_ref.shape[0]
    heads = q_ref.shape[1] // HD
    cols = query_rows * heads
    parts = key_rows // chunk
    scale = 1.0 / math.sqrt(HD)
    factor = scale * math.log2(math.e)
    me = lax.axis_index("ctx")
    chip = me // CORES
    core = me % CORES
    side = chip * CORES + (1 - core)
    is_top = chip == chips - 1
    not_top = chip < chips - 1
    has_low = chip > 0
    own_slot = me
    reach_ranks = max(look, CORES)

    barrier = pltpu.get_barrier_semaphore()
    there = jnp.int32(0)
    for d in range(1, reach_ranks + 1):
        @pl.when(me + d < ranks)
        def _():
            pl.semaphore_signal(barrier, inc=1, device_id={"ctx": me + d},
                                device_id_type=pl.DeviceIdType.MESH)

        @pl.when(me - d >= 0)
        def _():
            pl.semaphore_signal(barrier, inc=1, device_id={"ctx": me - d},
                                device_id_type=pl.DeviceIdType.MESH)

        there = there + jnp.where(me + d < ranks, 1, 0) + jnp.where(me - d >= 0, 1, 0)
    kbuf[own_slot] = k_ref[...]
    vbuf[own_slot] = v_ref[...]
    pl.semaphore_wait(barrier, there)

    def up(buf, sems, recv, w):
        slot = w * CORES + core
        return push(buf.at[slot], buf.at[slot], sems.at[w], recv.at[slot], me + CORES)

    def across(buf, sems, recv, w):
        slot = w * CORES + core
        return push(buf.at[slot], buf.at[slot], sems.at[w], recv.at[slot], side)

    def down(buf, sems, recv):
        return push(buf.at[own_slot], buf.at[own_slot], sems.at[0], recv.at[own_slot], me - CORES)

    def arrived(buf, sems, recv, slot):
        push(buf.at[slot], buf.at[slot], sems.at[0], recv.at[slot], side).wait_recv()

    def seg_copy(d, rank):
        return push(seg_ref, segs.at[d - 1], seg_send.at[d - 1], seg_recv.at[d - 1], rank)

    def grad_side(kind, w):
        return push(sib_out.at[kind, w], sib_in.at[kind, w], gs_send.at[kind, w], gs_recv.at[kind, w], side)

    def grad_down(kind, w):
        return push(ch_out.at[kind, w], ch_in.at[kind, w], gc_send.at[kind, w], gc_recv.at[kind, w], me - CORES)

    def grad_up(kind):
        return push(ch_out.at[kind, chip + 1], low_in.at[kind], gl_send.at[kind], gl_recv.at[kind], me + CORES)

    @pl.when(not_top)
    def _():
        up(kbuf, k_up, k_recv, chip).start()

    across(kbuf, k_side, k_recv, chip).start()
    for d in range(1, look + 1):
        @pl.when(me - d >= 0)
        def _():
            seg_copy(d, me - d).start()

    @pl.when(has_low)
    def _():
        down(kbuf, k_down, k_recv).start()
        down(vbuf, v_down, v_recv).start()

    across(vbuf, v_side, v_recv, chip).start()

    for h in range(heads):
        at = slice(h * HD, (h + 1) * HD)
        rows = slice(h * query_rows, (h + 1) * query_rows)
        q_h = q_ref[:, at]
        do_h = do_ref[:, at]
        qrows[rows, :] = q_h
        dorows[rows, :] = do_h
        qcols[:, rows] = q_h.T
        docols[:, rows] = do_h.T
        odot[:, rows] = jnp.sum((do_h.astype(F32) * o_ref[:, at].astype(F32)).T, axis=0, keepdims=True)
    top[...] = jnp.full(top.shape, FLOOR, F32)
    total[...] = jnp.zeros(total.shape, F32)
    dqt[...] = jnp.zeros(dqt.shape, F32)

    for d in range(1, look + 1):
        @pl.when(me + d < ranks)
        def _():
            seg_copy(d, side).wait_recv()

        @pl.when(me + d >= ranks)
        def _():
            segs[d - 1] = jnp.full(seg_ref.shape, 1 << 20, jnp.int32)

    seg_q = seg_ref[:, key_rows - query_rows:].astype(F32)
    seg_col = jnp.broadcast_to(seg_q, (HD, query_rows)).T
    counts = jnp.zeros((query_rows, HD), F32)
    for d in range(look + 1):
        for j in range(key_rows // HD):
            at = slice(j * HD, (j + 1) * HD)
            piece = (seg_ref[:, at] if d == 0 else segs[d - 1, :, at]).astype(F32)
            counts = counts + jnp.where(piece <= seg_col, 1.0, 0.0)
    count = jnp.sum(counts, axis=1, keepdims=True)
    segments = flag_ref.shape[1]
    ids = lax.broadcasted_iota(jnp.int32, (query_rows, segments), 1).astype(F32)
    flags = jnp.broadcast_to(flag_ref[...].astype(F32), (query_rows, segments))
    framed = jnp.sum(jnp.where(ids == seg_col[:, :1], flags, 0.0), axis=1, keepdims=True)
    local = (key_rows - query_rows) + lax.broadcasted_iota(jnp.int32, (query_rows, 1), 0).astype(F32)
    last = jnp.where(framed == 1.0, count - 1.0, local)
    last_row = jnp.broadcast_to(last, (query_rows, HD)).T[:1, :].astype(jnp.int32) + me * key_rows
    for h in range(heads):
        reach[:, h * query_rows:(h + 1) * query_rows] = last_row

    def rows_of(part):
        return pl.ds(pl.multiple_of(part * chunk, chunk), chunk)

    def scores_of(slot, part, masked):
        s = jnp.dot(kbuf[slot, rows_of(part), :], qcols[...], preferred_element_type=F32) * factor
        if masked:
            first = slot * key_rows + part * chunk
            pos = first + lax.broadcasted_iota(jnp.int32, (chunk, cols), 0)
            s = jnp.where(pos <= reach[...], s, LOW)
        return s

    def stats(slot, masked):
        @pl.loop(0, parts)
        def _(part):
            s = scores_of(slot, part, masked)
            here = jnp.maximum(jnp.max(s, axis=0, keepdims=True), FLOOR)
            e = jnp.exp2(s - here)
            if keep:
                ebuf[slot, rows_of(part), :] = e
                tops[slot * parts + part] = here
            old = top[...]
            new = jnp.maximum(old, here)
            total[...] = total[...] * jnp.exp2(old - new) + (
                jnp.sum(e, axis=0, keepdims=True) * jnp.exp2(here - new))
            top[...] = new

    def chip_stats(w, masked):
        @pl.loop(0, CORES)
        def _(b):
            slot = w * CORES + (core + b) % CORES

            @pl.when(b == 1)
            def _():
                arrived(kbuf, k_side, k_recv, slot)

            stats(slot, masked)

    def probs_of(slot, part, masked):
        if keep:
            return ebuf[slot, rows_of(part), :] * jnp.exp2(tops[slot * parts + part] - lse[...])
        return jnp.exp2(scores_of(slot, part, masked) - lse[...])

    def send_side(kind, w):
        sib_out[kind, w] = gpart[kind, w * CORES + (1 - core)].astype(BF16)
        grad_side(kind, w).start()

    def value_grads(w, masked):
        @pl.loop(0, CORES * parts)
        def _(i):
            slot = w * CORES + i // parts
            part = i % parts
            p = probs_of(slot, part, masked).astype(BF16)
            gpart[0, slot, rows_of(part), :] = jnp.dot(p, dorows[...], preferred_element_type=F32)

        send_side(0, w)

    def key_grads(w, masked):
        @pl.loop(0, CORES)
        def _(b):
            slot = w * CORES + (core + b) % CORES

            @pl.when(b == 1)
            def _():
                arrived(vbuf, v_side, v_recv, slot)

            @pl.loop(0, parts)
            def _(part):
                p = probs_of(slot, part, masked)
                dp = jnp.dot(vbuf[slot, rows_of(part), :], docols[...], preferred_element_type=F32)
                ds = (p * (dp - odot[...])).astype(BF16)
                gpart[1, slot, rows_of(part), :] = scale * jnp.dot(ds, qrows[...], preferred_element_type=F32)
                dqt[...] += jnp.dot(kbuf[slot, rows_of(part), :].T, ds, preferred_element_type=F32)

        send_side(1, w)

    def summed(kind, w):
        grad_side(kind, w).wait_recv()
        return gpart[kind, w * CORES + core] + sib_in[kind, w].astype(F32)

    def hand_down(kind, w):
        mine = gpart.at[kind, w * CORES + core]
        mine[...] = summed(kind, w)

        @pl.when(not_top)
        def _():
            grad_down(kind, w).wait_recv()
            mine[...] += ch_in[kind, w].astype(F32)

        ch_out[kind, w] = mine[...].astype(BF16)
        grad_down(kind, w).start()

    @pl.when(jnp.logical_and(not_top, chip == 0))
    def _():
        up(vbuf, v_up, v_recv, chip).start()

    chip_stats(chip, True)

    @pl.loop(1, chip + 1)
    def _(s):
        w = chip - s
        arrived(kbuf, k_side, k_recv, w * CORES + core)

        @pl.when(not_top)
        def _():
            up(kbuf, k_up, k_recv, w).start()

        across(kbuf, k_side, k_recv, w).start()

        @pl.when(jnp.logical_and(not_top, w == 0))
        def _():
            up(vbuf, v_up, v_recv, chip).start()

        chip_stats(w, False)

    @pl.when(not_top)
    def _():
        arrived(kbuf, k_side, k_recv, (chip + 1) * CORES + core)
        across(kbuf, k_side, k_recv, chip + 1).start()
        chip_stats(chip + 1, True)

    lse[...] = top[...] + jnp.log(total[...]) * math.log2(math.e)

    @pl.loop(0, chip)
    def _(t):
        w = chip - 1 - t
        value_grads(w, False)

        @pl.when(not_top)
        def _():
            arrived(vbuf, v_side, v_recv, w * CORES + core)
            up(vbuf, v_up, v_recv, w).start()
            across(vbuf, v_side, v_recv, w).start()

        @pl.when(jnp.logical_and(is_top, t > 0))
        def _():
            hand_down(0, w + 1)

    @pl.when(jnp.logical_and(is_top, has_low))
    def _():
        hand_down(0, 0)

    @pl.loop(0, chip)
    def _(t):
        w = chip - 1 - t

        @pl.when(is_top)
        def _():
            arrived(vbuf, v_side, v_recv, w * CORES + core)
            across(vbuf, v_side, v_recv, w).start()

        key_grads(w, False)

        @pl.when(jnp.logical_and(is_top, t > 0))
        def _():
            hand_down(1, w + 1)

        @pl.when(not_top)
        def _():
            hand_down(0, w)

    @pl.when(jnp.logical_and(is_top, has_low))
    def _():
        hand_down(1, 0)

    end = jnp.where(not_top, 2, 1)

    @pl.loop(0, end)
    def _(t):
        w = chip + end - 1 - t

        @pl.when(jnp.logical_and(not_top, w == chip))
        def _():
            @pl.loop(0, chip)
            def _(s):
                hand_down(1, chip - 1 - s)

        value_grads(w, True)

        @pl.when(w > chip)
        def _():
            arrived(vbuf, v_side, v_recv, w * CORES + core)
            across(vbuf, v_side, v_recv, w).start()

        key_grads(w, True)

        @pl.when(w > chip)
        def _():
            for kind in range(2):
                ch_out[kind, w] = summed(kind, w).astype(BF16)
                grad_up(kind).start()

    for h in range(heads):
        rows = slice(h * query_rows, (h + 1) * query_rows)
        dq_ref[:, h * HD:(h + 1) * HD] = (dqt[:, rows].T * scale).astype(BF16)

    for kind, out in ((0, dv_ref), (1, dk_ref)):
        gpart[kind, own_slot] = summed(kind, chip)

        @pl.when(has_low)
        def _():
            push(low_in.at[kind], low_in.at[kind], gl_send.at[kind], gl_recv.at[kind], side).wait_recv()
            gpart[kind, own_slot] = gpart[kind, own_slot] + low_in[kind].astype(F32)

        @pl.when(not_top)
        def _():
            grad_down(kind, chip).wait_recv()
            gpart[kind, own_slot] = gpart[kind, own_slot] + ch_in[kind, chip].astype(F32)

        out[...] = gpart[kind, own_slot].astype(BF16)

    for d in range(1, look + 1):
        @pl.when(me - d >= 0)
        def _():
            seg_copy(d, side).wait_send()

    @pl.when(has_low)
    def _():
        down(kbuf, k_down, k_recv).wait_send()
        down(vbuf, v_down, v_recv).wait_send()

    @pl.when(not_top)
    def _():
        for kind in range(2):
            grad_up(kind).wait_send()

    @pl.loop(0, chip + end)
    def _(w):
        across(kbuf, k_side, k_recv, w).wait_send()
        across(vbuf, v_side, v_recv, w).wait_send()
        for kind in range(2):
            grad_side(kind, w).wait_send()

        @pl.when(jnp.logical_and(not_top, w <= chip))
        def _():
            up(kbuf, k_up, k_recv, w).wait_send()
            up(vbuf, v_up, v_recv, w).wait_send()

        @pl.when(w < chip)
        def _():
            for kind in range(2):
                grad_down(kind, w).wait_send()


def per_device(queries, keys, values, grad_out, saved_out, segment_ids, frame_flags):
    ranks = lax.axis_size("ctx")
    chips = ranks // CORES
    key_rows = keys.shape[1]
    query_rows, width = queries.shape[1:]
    cols = query_rows * (width // HD)
    look = (SEG_MOST + key_rows - 2) // key_rows
    assert look <= CORES and ranks % CORES == 0
    chunk = math.gcd(key_rows, 512)
    parts = key_rows // chunk
    keep = ranks * key_rows * cols * 4 <= KEEP_BYTES
    kept = ranks if keep else 1
    dma = pltpu.SemaphoreType.DMA
    block = (key_rows, HD)
    grads = (2, chips) + block
    vmem = pl.BlockSpec(memory_space=pltpu.VMEM)
    grad_queries, grad_keys, grad_values = pl.pallas_call(
        functools.partial(fused, ranks, look, chunk, keep),
        out_shape=(
            jax.ShapeDtypeStruct((query_rows, width), BF16),
            jax.ShapeDtypeStruct(block, BF16),
            jax.ShapeDtypeStruct(block, BF16),
        ),
        in_specs=[vmem] * 7,
        out_specs=(vmem,) * 3,
        scratch_shapes=[
            pltpu.VMEM((ranks,) + block, BF16),
            pltpu.VMEM((ranks,) + block, BF16),
            pltpu.VMEM((kept, key_rows, cols), F32) if keep else pltpu.VMEM((8, 128), F32),
            pltpu.VMEM((kept * parts, 1, cols), F32),
            pltpu.VMEM((HD, cols), BF16),
            pltpu.VMEM((cols, HD), BF16),
            pltpu.VMEM((HD, cols), BF16),
            pltpu.VMEM((cols, HD), BF16),
            pltpu.VMEM((1, cols), jnp.int32),
            pltpu.VMEM((1, cols), F32),
            pltpu.VMEM((1, cols), F32),
            pltpu.VMEM((1, cols), F32),
            pltpu.VMEM((1, cols), F32),
            pltpu.VMEM((HD, cols), F32),
            pltpu.VMEM((2, ranks) + block, F32),
            pltpu.VMEM(grads, BF16),
            pltpu.VMEM(grads, BF16),
            pltpu.VMEM(grads, BF16),
            pltpu.VMEM(grads, BF16),
            pltpu.VMEM((2,) + block, BF16),
            pltpu.VMEM((look, 1, key_rows), jnp.int32),
            dma((chips,)), dma((chips,)), dma((1,)), dma((ranks,)),
            dma((chips,)), dma((chips,)), dma((1,)), dma((ranks,)),
            dma((2, chips)), dma((2, chips)), dma((2, chips)), dma((2, chips)),
            dma((2,)), dma((2,)), dma((look,)), dma((look,)),
        ],
        compiler_params=pltpu.CompilerParams(
            collective_id=0, has_side_effects=True, vmem_limit_bytes=60 * 1024 * 1024
        ),
        cost_estimate=pl.CostEstimate(
            flops=12 * cols * ranks * key_rows * HD,
            bytes_accessed=8 * cols * HD,
            transcendentals=cols * ranks * key_rows,
        ),
    )(queries[0], keys[0], values[0], grad_out[0], saved_out[0], segment_ids, frame_flags)
    return grad_queries[None], grad_keys[None], grad_values[None]


def solution(mesh):
    return jax.shard_map(
        per_device,
        mesh=mesh,
        in_specs=(
            P("dp", "ctx", None),
            P("dp", "ctx", None),
            P("dp", "ctx", None),
            P("dp", "ctx", None),
            P("dp", "ctx", None),
            P("dp", "ctx"),
            P("dp", None),
        ),
        out_specs=(P("dp", "ctx", None), P("dp", "ctx", None), P("dp", "ctx", None)),
        check_vma=False,
    )
```

```python
import functools
import math

import jax
import jax.numpy as jnp
from jax import lax
from jax.experimental import pallas as pl
from jax.experimental.pallas import tpu as pltpu
from jax.sharding import PartitionSpec as P

HD = 128
SEG_MOST = 1024
CORES = 2
LOW = -1e30
FLOOR = -1e29
KEEP_BYTES = 20 * 1024 * 1024
F32 = jnp.float32
BF16 = jnp.bfloat16


def push(src, dst, send, recv, rank):
    return pltpu.make_async_remote_copy(
        src_ref=src,
        dst_ref=dst,
        send_sem=send,
        recv_sem=recv,
        device_id={"ctx": rank},
        device_id_type=pl.DeviceIdType.MESH,
    )


def fused(
    ranks, look, chunk, keep,
    q_ref, k_ref, v_ref, do_ref, o_ref, seg_ref, flag_ref,
    dq_ref, dk_ref, dv_ref,
    kbuf, vbuf, ebuf, tops, qcols, qrows, docols, dorows, reach, odot, top, total, lse, dqt,
    low, gpart, sib_out, sib_in, ch_out, ch_in, low_in, segs,
    k_up, k_side, k_down, k_recv, v_up, v_side, v_down, v_recv,
    gs_send, gs_recv, gc_send, gc_recv, gl_send, gl_recv, seg_send, seg_recv,
):
    chips = ranks // CORES
    key_rows = k_ref.shape[0]
    query_rows = q_ref.shape[0]
    heads = q_ref.shape[1] // HD
    cols = query_rows * heads
    parts = key_rows // chunk
    strip = math.gcd(cols, 256)
    piece = math.gcd(chunk, 64)
    scale = 1.0 / math.sqrt(HD)
    factor = scale * math.log2(math.e)
    me = lax.axis_index("ctx")
    chip = me // CORES
    core = me % CORES
    side = chip * CORES + (1 - core)
    is_top = chip == chips - 1
    not_top = chip < chips - 1
    has_low = chip > 0
    own_slot = me
    reach_ranks = max(look, CORES)

    barrier = pltpu.get_barrier_semaphore()
    there = jnp.int32(0)
    for d in range(1, reach_ranks + 1):
        @pl.when(me + d < ranks)
        def _():
            pl.semaphore_signal(barrier, inc=1, device_id={"ctx": me + d},
                                device_id_type=pl.DeviceIdType.MESH)

        @pl.when(me - d >= 0)
        def _():
            pl.semaphore_signal(barrier, inc=1, device_id={"ctx": me - d},
                                device_id_type=pl.DeviceIdType.MESH)

        there = there + jnp.where(me + d < ranks, 1, 0) + jnp.where(me - d >= 0, 1, 0)
    kbuf[own_slot] = k_ref[...]
    vbuf[own_slot] = v_ref[...]
    pl.semaphore_wait(barrier, there)

    def up(buf, sems, recv, w):
        slot = w * CORES + core
        return push(buf.at[slot], buf.at[slot], sems.at[w], recv.at[slot], me + CORES)

    def across(buf, sems, recv, w):
        slot = w * CORES + core
        return push(buf.at[slot], buf.at[slot], sems.at[w], recv.at[slot], side)

    def down(buf, sems, recv):
        return push(buf.at[own_slot], buf.at[own_slot], sems.at[0], recv.at[own_slot], me - CORES)

    def arrived(buf, sems, recv, slot):
        push(buf.at[slot], buf.at[slot], sems.at[0], recv.at[slot], side).wait_recv()

    def seg_copy(d, rank):
        return push(seg_ref, segs.at[d - 1], seg_send.at[d - 1], seg_recv.at[d - 1], rank)

    def grad_side(kind, w):
        return push(sib_out.at[kind, w], sib_in.at[kind, w], gs_send.at[kind, w], gs_recv.at[kind, w], side)

    def grad_down(kind, w):
        return push(ch_out.at[kind, w], ch_in.at[kind, w], gc_send.at[kind, w], gc_recv.at[kind, w], me - CORES)

    def grad_up(kind):
        return push(ch_out.at[kind, chip + 1], low_in.at[kind], gl_send.at[kind], gl_recv.at[kind], me + CORES)

    @pl.when(not_top)
    def _():
        up(kbuf, k_up, k_recv, chip).start()

    across(kbuf, k_side, k_recv, chip).start()
    for d in range(1, look + 1):
        @pl.when(me - d >= 0)
        def _():
            seg_copy(d, me - d).start()

    @pl.when(has_low)
    def _():
        down(kbuf, k_down, k_recv).start()
        down(vbuf, v_down, v_recv).start()

    across(vbuf, v_side, v_recv, chip).start()

    for h in range(heads):
        at = slice(h * HD, (h + 1) * HD)
        rows = slice(h * query_rows, (h + 1) * query_rows)
        q_h = q_ref[:, at]
        do_h = do_ref[:, at]
        qrows[rows, :] = q_h
        dorows[rows, :] = do_h
        qcols[:, rows] = q_h.T
        docols[:, rows] = do_h.T
        odot[:, rows] = jnp.sum((do_h.astype(F32) * o_ref[:, at].astype(F32)).T, axis=0, keepdims=True)
    top[...] = jnp.full(top.shape, FLOOR, F32)
    total[...] = jnp.zeros(total.shape, F32)
    dqt[...] = jnp.zeros(dqt.shape, F32)

    for d in range(1, look + 1):
        @pl.when(me + d < ranks)
        def _():
            seg_copy(d, side).wait_recv()

        @pl.when(me + d >= ranks)
        def _():
            segs[d - 1] = jnp.full(seg_ref.shape, 1 << 20, jnp.int32)

    seg_q = seg_ref[:, key_rows - query_rows:].astype(F32)
    seg_col = jnp.broadcast_to(seg_q, (HD, query_rows)).T
    counts = jnp.zeros((query_rows, HD), F32)
    for d in range(look + 1):
        for j in range(key_rows // HD):
            at = slice(j * HD, (j + 1) * HD)
            ids_row = (seg_ref[:, at] if d == 0 else segs[d - 1, :, at]).astype(F32)
            counts = counts + jnp.where(ids_row <= seg_col, 1.0, 0.0)
    count = jnp.sum(counts, axis=1, keepdims=True)
    segments = flag_ref.shape[1]
    ids = lax.broadcasted_iota(jnp.int32, (query_rows, segments), 1).astype(F32)
    flags = jnp.broadcast_to(flag_ref[...].astype(F32), (query_rows, segments))
    framed = jnp.sum(jnp.where(ids == seg_col[:, :1], flags, 0.0), axis=1, keepdims=True)
    local = (key_rows - query_rows) + lax.broadcasted_iota(jnp.int32, (query_rows, 1), 0).astype(F32)
    last = jnp.where(framed == 1.0, count - 1.0, local)
    last_row = jnp.broadcast_to(last, (query_rows, HD)).T[:1, :].astype(jnp.int32) + me * key_rows
    for h in range(heads):
        reach[:, h * query_rows:(h + 1) * query_rows] = last_row

    def rows_of(part):
        return pl.ds(pl.multiple_of(part * chunk, chunk), chunk)

    def masked_scores(slot, part, at, masked):
        s = jnp.dot(kbuf[slot, rows_of(part), :], qcols[:, at], preferred_element_type=F32)
        if masked:
            first = slot * key_rows + part * chunk
            pos = first + lax.broadcasted_iota(jnp.int32, s.shape, 0)
            s = jnp.where(pos <= reach[:, at], s, LOW)
        return s

    strips = [slice(i, i + strip) for i in range(0, cols, strip)]
    slices = [slice(i, i + piece) for i in range(0, chunk, piece)]

    def slice_of(part, rows):
        return pl.ds(pl.multiple_of(part * chunk + rows.start, piece), piece)

    def stats(slot, masked):
        @pl.loop(0, parts)
        def _(part):
            for at in strips:
                s = masked_scores(slot, part, at, masked)
                here = jnp.maximum(jnp.max(s, axis=0, keepdims=True), FLOOR)
                added = jnp.zeros((1, strip), F32)
                for rows in slices:
                    e = jnp.exp2((s[rows] - here) * factor)
                    if keep:
                        ebuf[slot, slice_of(part, rows), at] = e
                    added = added + jnp.sum(e, axis=0, keepdims=True)
                here = here * factor
                if keep:
                    tops[slot * parts + part, :, at] = here
                old = top[:, at]
                new = jnp.maximum(old, here)
                total[:, at] = total[:, at] * jnp.exp2(old - new) + added * jnp.exp2(here - new)
                top[:, at] = new

    def chip_stats(w, masked):
        @pl.loop(0, CORES)
        def _(b):
            slot = w * CORES + (core + b) % CORES

            @pl.when(b == 1)
            def _():
                arrived(kbuf, k_side, k_recv, slot)

            stats(slot, masked)

    def probs_of(slot, part, at, masked):
        if keep:
            level = jnp.exp2(tops[slot * parts + part, :, at] - lse[:, at])
            return lambda rows: ebuf[slot, slice_of(part, rows), at] * level
        s = masked_scores(slot, part, at, masked)
        return lambda rows: jnp.exp2(s[rows] * factor - lse[:, at])

    def send_side(kind, w):
        sib_out[kind, w] = gpart[kind, w * CORES + (1 - core)].astype(BF16)
        grad_side(kind, w).start()

    def value_grads(w, masked):
        @pl.loop(0, CORES * parts)
        def _(i):
            slot = w * CORES + i // parts
            part = i % parts
            for at in strips:
                probs = probs_of(slot, part, at, masked)
                for rows in slices:
                    low[rows, at] = probs(rows).astype(BF16)
            gpart[0, slot, rows_of(part), :] = jnp.dot(low[...], dorows[...], preferred_element_type=F32)

        send_side(0, w)

    def key_grads(w, masked):
        @pl.loop(0, CORES)
        def _(b):
            slot = w * CORES + (core + b) % CORES

            @pl.when(b == 1)
            def _():
                arrived(vbuf, v_side, v_recv, slot)

            @pl.loop(0, parts)
            def _(part):
                keys_t = kbuf[slot, rows_of(part), :].T
                for at in strips:
                    probs = probs_of(slot, part, at, masked)
                    dp = jnp.dot(vbuf[slot, rows_of(part), :], docols[:, at], preferred_element_type=F32)
                    for rows in slices:
                        low[rows, at] = (probs(rows) * (dp[rows] - odot[:, at])).astype(BF16)
                    dqt[:, at] += jnp.dot(keys_t, low[:, at], preferred_element_type=F32)
                gpart[1, slot, rows_of(part), :] = scale * jnp.dot(low[...], qrows[...], preferred_element_type=F32)

        send_side(1, w)

    def summed(kind, w):
        grad_side(kind, w).wait_recv()
        return gpart[kind, w * CORES + core] + sib_in[kind, w].astype(F32)

    def hand_down(kind, w):
        mine = gpart.at[kind, w * CORES + core]
        mine[...] = summed(kind, w)

        @pl.when(not_top)
        def _():
            grad_down(kind, w).wait_recv()
            mine[...] += ch_in[kind, w].astype(F32)

        ch_out[kind, w] = mine[...].astype(BF16)
        grad_down(kind, w).start()

    @pl.when(jnp.logical_and(not_top, chip == 0))
    def _():
        up(vbuf, v_up, v_recv, chip).start()

    chip_stats(chip, True)

    @pl.loop(1, chip + 1)
    def _(s):
        w = chip - s
        arrived(kbuf, k_side, k_recv, w * CORES + core)

        @pl.when(not_top)
        def _():
            up(kbuf, k_up, k_recv, w).start()

        across(kbuf, k_side, k_recv, w).start()

        @pl.when(jnp.logical_and(not_top, w == 0))
        def _():
            up(vbuf, v_up, v_recv, chip).start()

        chip_stats(w, False)

    @pl.when(not_top)
    def _():
        arrived(kbuf, k_side, k_recv, (chip + 1) * CORES + core)
        across(kbuf, k_side, k_recv, chip + 1).start()
        chip_stats(chip + 1, True)

    lse[...] = top[...] + jnp.log(total[...]) * math.log2(math.e)

    @pl.loop(0, chip)
    def _(t):
        w = chip - 1 - t
        value_grads(w, False)

        @pl.when(not_top)
        def _():
            arrived(vbuf, v_side, v_recv, w * CORES + core)
            up(vbuf, v_up, v_recv, w).start()
            across(vbuf, v_side, v_recv, w).start()

        @pl.when(jnp.logical_and(is_top, t > 0))
        def _():
            hand_down(0, w + 1)

    @pl.when(jnp.logical_and(is_top, has_low))
    def _():
        hand_down(0, 0)

    @pl.loop(0, chip)
    def _(t):
        w = chip - 1 - t

        @pl.when(is_top)
        def _():
            arrived(vbuf, v_side, v_recv, w * CORES + core)
            across(vbuf, v_side, v_recv, w).start()

        key_grads(w, False)

        @pl.when(jnp.logical_and(is_top, t > 0))
        def _():
            hand_down(1, w + 1)

        @pl.when(not_top)
        def _():
            hand_down(0, w)

    @pl.when(jnp.logical_and(is_top, has_low))
    def _():
        hand_down(1, 0)

    end = jnp.where(not_top, 2, 1)

    @pl.loop(0, end)
    def _(t):
        w = chip + end - 1 - t

        @pl.when(jnp.logical_and(not_top, w == chip))
        def _():
            @pl.loop(0, chip)
            def _(s):
                hand_down(1, chip - 1 - s)

        value_grads(w, True)

        @pl.when(w > chip)
        def _():
            arrived(vbuf, v_side, v_recv, w * CORES + core)
            across(vbuf, v_side, v_recv, w).start()

        key_grads(w, True)

        @pl.when(w > chip)
        def _():
            for kind in range(2):
                ch_out[kind, w] = summed(kind, w).astype(BF16)
                grad_up(kind).start()

    for h in range(heads):
        rows = slice(h * query_rows, (h + 1) * query_rows)
        dq_ref[:, h * HD:(h + 1) * HD] = (dqt[:, rows].T * scale).astype(BF16)

    for kind, out in ((0, dv_ref), (1, dk_ref)):
        gpart[kind, own_slot] = summed(kind, chip)

        @pl.when(has_low)
        def _():
            push(low_in.at[kind], low_in.at[kind], gl_send.at[kind], gl_recv.at[kind], side).wait_recv()
            gpart[kind, own_slot] = gpart[kind, own_slot] + low_in[kind].astype(F32)

        @pl.when(not_top)
        def _():
            grad_down(kind, chip).wait_recv()
            gpart[kind, own_slot] = gpart[kind, own_slot] + ch_in[kind, chip].astype(F32)

        out[...] = gpart[kind, own_slot].astype(BF16)

    for d in range(1, look + 1):
        @pl.when(me - d >= 0)
        def _():
            seg_copy(d, side).wait_send()

    @pl.when(has_low)
    def _():
        down(kbuf, k_down, k_recv).wait_send()
        down(vbuf, v_down, v_recv).wait_send()

    @pl.when(not_top)
    def _():
        for kind in range(2):
            grad_up(kind).wait_send()

    @pl.loop(0, chip + end)
    def _(w):
        across(kbuf, k_side, k_recv, w).wait_send()
        across(vbuf, v_side, v_recv, w).wait_send()
        for kind in range(2):
            grad_side(kind, w).wait_send()

        @pl.when(jnp.logical_and(not_top, w <= chip))
        def _():
            up(kbuf, k_up, k_recv, w).wait_send()
            up(vbuf, v_up, v_recv, w).wait_send()

        @pl.when(w < chip)
        def _():
            for kind in range(2):
                grad_down(kind, w).wait_send()


def per_device(queries, keys, values, grad_out, saved_out, segment_ids, frame_flags):
    ranks = lax.axis_size("ctx")
    chips = ranks // CORES
    key_rows = keys.shape[1]
    query_rows, width = queries.shape[1:]
    cols = query_rows * (width // HD)
    look = (SEG_MOST + key_rows - 2) // key_rows
    assert look <= CORES and ranks % CORES == 0
    chunk = math.gcd(key_rows, 512)
    parts = key_rows // chunk
    keep = ranks * key_rows * cols * 4 <= KEEP_BYTES
    kept = ranks if keep else 1
    dma = pltpu.SemaphoreType.DMA
    block = (key_rows, HD)
    grads = (2, chips) + block
    vmem = pl.BlockSpec(memory_space=pltpu.VMEM)
    grad_queries, grad_keys, grad_values = pl.pallas_call(
        functools.partial(fused, ranks, look, chunk, keep),
        out_shape=(
            jax.ShapeDtypeStruct((query_rows, width), BF16),
            jax.ShapeDtypeStruct(block, BF16),
            jax.ShapeDtypeStruct(block, BF16),
        ),
        in_specs=[vmem] * 7,
        out_specs=(vmem,) * 3,
        scratch_shapes=[
            pltpu.VMEM((ranks,) + block, BF16),
            pltpu.VMEM((ranks,) + block, BF16),
            pltpu.VMEM((kept, key_rows, cols), F32) if keep else pltpu.VMEM((8, 128), F32),
            pltpu.VMEM((kept * parts, 1, cols), F32),
            pltpu.VMEM((HD, cols), BF16),
            pltpu.VMEM((cols, HD), BF16),
            pltpu.VMEM((HD, cols), BF16),
            pltpu.VMEM((cols, HD), BF16),
            pltpu.VMEM((1, cols), jnp.int32),
            pltpu.VMEM((1, cols), F32),
            pltpu.VMEM((1, cols), F32),
            pltpu.VMEM((1, cols), F32),
            pltpu.VMEM((1, cols), F32),
            pltpu.VMEM((HD, cols), F32),
            pltpu.VMEM((chunk, cols), BF16),
            pltpu.VMEM((2, ranks) + block, F32),
            pltpu.VMEM(grads, BF16),
            pltpu.VMEM(grads, BF16),
            pltpu.VMEM(grads, BF16),
            pltpu.VMEM(grads, BF16),
            pltpu.VMEM((2,) + block, BF16),
            pltpu.VMEM((look, 1, key_rows), jnp.int32),
            dma((chips,)), dma((chips,)), dma((1,)), dma((ranks,)),
            dma((chips,)), dma((chips,)), dma((1,)), dma((ranks,)),
            dma((2, chips)), dma((2, chips)), dma((2, chips)), dma((2, chips)),
            dma((2,)), dma((2,)), dma((look,)), dma((look,)),
        ],
        compiler_params=pltpu.CompilerParams(
            collective_id=0, has_side_effects=True, vmem_limit_bytes=60 * 1024 * 1024
        ),
        cost_estimate=pl.CostEstimate(
            flops=12 * cols * ranks * key_rows * HD,
            bytes_accessed=8 * cols * HD,
            transcendentals=cols * ranks * key_rows,
        ),
    )(queries[0], keys[0], values[0], grad_out[0], saved_out[0], segment_ids, frame_flags)
    return grad_queries[None], grad_keys[None], grad_values[None]


def solution(mesh):
    return jax.shard_map(
        per_device,
        mesh=mesh,
        in_specs=(
            P("dp", "ctx", None),
            P("dp", "ctx", None),
            P("dp", "ctx", None),
            P("dp", "ctx", None),
            P("dp", "ctx", None),
            P("dp", "ctx"),
            P("dp", None),
        ),
        out_specs=(P("dp", "ctx", None), P("dp", "ctx", None), P("dp", "ctx", None)),
        check_vma=False,
    )
```

```python
import functools
import math

import jax
import jax.numpy as jnp
from jax import lax
from jax.experimental import pallas as pl
from jax.experimental.pallas import tpu as pltpu
from jax.sharding import PartitionSpec as P

HD = 128
SEG_MOST = 1024
CORES = 2
HALVES = 2
LOW = -1e30
FLOOR = -1e29
KEEP_BYTES = 20 * 1024 * 1024
F32 = jnp.float32
BF16 = jnp.bfloat16


def push(src, dst, send, recv, rank):
    return pltpu.make_async_remote_copy(
        src_ref=src,
        dst_ref=dst,
        send_sem=send,
        recv_sem=recv,
        device_id={"ctx": rank},
        device_id_type=pl.DeviceIdType.MESH,
    )


def fused(
    ranks, look, chunk, keep,
    q_ref, k_ref, v_ref, do_ref, o_ref, seg_ref, flag_ref,
    dq_ref, dk_ref, dv_ref,
    kbuf, vbuf, ebuf, tops, qcols, qrows, docols, dorows, reach, odot, top, total, lse, dqt,
    gpart, sib_out, sib_in, ch_out, ch_in, low_in, segs,
    k_up, k_low, k_side, k_down, k_recv, v_up, v_low, v_side, v_down, v_recv,
    gs_send, gs_recv, gc_send, gc_recv, gl_send, gl_recv, seg_send, seg_recv,
):
    chips = ranks // CORES
    key_rows = k_ref.shape[0]
    query_rows = q_ref.shape[0]
    heads = q_ref.shape[1] // HD
    cols = query_rows * heads
    parts = key_rows // chunk
    scale = 1.0 / math.sqrt(HD)
    factor = scale * math.log2(math.e)
    me = lax.axis_index("ctx")
    chip = me // CORES
    core = me % CORES
    side = chip * CORES + (1 - core)
    is_top = chip == chips - 1
    not_top = chip < chips - 1
    has_low = chip > 0
    own_slot = me
    reach_ranks = max(look, CORES)

    barrier = pltpu.get_barrier_semaphore()
    there = jnp.int32(0)
    for d in range(1, reach_ranks + 1):
        @pl.when(me + d < ranks)
        def _():
            pl.semaphore_signal(barrier, inc=1, device_id={"ctx": me + d},
                                device_id_type=pl.DeviceIdType.MESH)

        @pl.when(me - d >= 0)
        def _():
            pl.semaphore_signal(barrier, inc=1, device_id={"ctx": me - d},
                                device_id_type=pl.DeviceIdType.MESH)

        there = there + jnp.where(me + d < ranks, 1, 0) + jnp.where(me - d >= 0, 1, 0)
    kbuf[own_slot] = k_ref[...]
    vbuf[own_slot] = v_ref[...]
    pl.semaphore_wait(barrier, there)

    def up(buf, sems, recv, w, half, rank):
        rows = pl.ds(half * (key_rows // HALVES), key_rows // HALVES)
        place = buf.at[w * CORES + core, rows]
        return push(place, place, sems.at[w, half], recv.at[w, half], rank)

    def start_up(buf, sems, recv, w):
        for half in range(HALVES):
            up(buf, sems, recv, w, half, me + CORES).start()

    def from_below(buf, sems, recv, w, forward):
        for half in range(HALVES):
            up(buf, sems, recv, w, half, side).wait_recv()
            if forward:
                up(buf, sems, recv, w, half, me + CORES).start()

    def across(buf, sems, recv, w):
        slot = w * CORES + core
        return push(buf.at[slot], buf.at[slot], sems.at[w], recv.at[slot], side)

    def down(buf, sems, recv):
        return push(buf.at[own_slot], buf.at[own_slot], sems.at[0], recv.at[own_slot], me - CORES)

    def arrived(buf, sems, recv, slot):
        push(buf.at[slot], buf.at[slot], sems.at[0], recv.at[slot], side).wait_recv()

    def seg_copy(d, rank):
        return push(seg_ref, segs.at[d - 1], seg_send.at[d - 1], seg_recv.at[d - 1], rank)

    def grad_side(kind, w):
        return push(sib_out.at[kind, w], sib_in.at[kind, w], gs_send.at[kind, w], gs_recv.at[kind, w], side)

    def grad_down(kind, w):
        return push(ch_out.at[kind, w], ch_in.at[kind, w], gc_send.at[kind, w], gc_recv.at[kind, w], me - CORES)

    def grad_up(kind):
        return push(ch_out.at[kind, chip + 1], low_in.at[kind], gl_send.at[kind], gl_recv.at[kind], me + CORES)

    @pl.when(not_top)
    def _():
        start_up(kbuf, k_up, k_low, chip)

    across(kbuf, k_side, k_recv, chip).start()
    for d in range(1, look + 1):
        @pl.when(me - d >= 0)
        def _():
            seg_copy(d, me - d).start()

    @pl.when(has_low)
    def _():
        down(kbuf, k_down, k_recv).start()
        down(vbuf, v_down, v_recv).start()

    across(vbuf, v_side, v_recv, chip).start()

    for h in range(heads):
        at = slice(h * HD, (h + 1) * HD)
        rows = slice(h * query_rows, (h + 1) * query_rows)
        q_h = q_ref[:, at]
        do_h = do_ref[:, at]
        qrows[rows, :] = q_h
        dorows[rows, :] = do_h
        qcols[:, rows] = q_h.T
        docols[:, rows] = do_h.T
        odot[:, rows] = jnp.sum((do_h.astype(F32) * o_ref[:, at].astype(F32)).T, axis=0, keepdims=True)
    top[...] = jnp.full(top.shape, FLOOR, F32)
    total[...] = jnp.zeros(total.shape, F32)
    dqt[...] = jnp.zeros(dqt.shape, F32)

    for d in range(1, look + 1):
        @pl.when(me + d < ranks)
        def _():
            seg_copy(d, side).wait_recv()

        @pl.when(me + d >= ranks)
        def _():
            segs[d - 1] = jnp.full(seg_ref.shape, 1 << 20, jnp.int32)

    seg_q = seg_ref[:, key_rows - query_rows:].astype(F32)
    seg_col = jnp.broadcast_to(seg_q, (HD, query_rows)).T
    counts = jnp.zeros((query_rows, HD), F32)
    for d in range(look + 1):
        for j in range(key_rows // HD):
            at = slice(j * HD, (j + 1) * HD)
            piece = (seg_ref[:, at] if d == 0 else segs[d - 1, :, at]).astype(F32)
            counts = counts + jnp.where(piece <= seg_col, 1.0, 0.0)
    count = jnp.sum(counts, axis=1, keepdims=True)
    segments = flag_ref.shape[1]
    ids = lax.broadcasted_iota(jnp.int32, (query_rows, segments), 1).astype(F32)
    flags = jnp.broadcast_to(flag_ref[...].astype(F32), (query_rows, segments))
    framed = jnp.sum(jnp.where(ids == seg_col[:, :1], flags, 0.0), axis=1, keepdims=True)
    local = (key_rows - query_rows) + lax.broadcasted_iota(jnp.int32, (query_rows, 1), 0).astype(F32)
    last = jnp.where(framed == 1.0, count - 1.0, local)
    last_row = jnp.broadcast_to(last, (query_rows, HD)).T[:1, :].astype(jnp.int32) + me * key_rows
    for h in range(heads):
        reach[:, h * query_rows:(h + 1) * query_rows] = last_row

    def rows_of(part):
        return pl.ds(pl.multiple_of(part * chunk, chunk), chunk)

    def scores_of(slot, part, masked):
        s = jnp.dot(kbuf[slot, rows_of(part), :], qcols[...], preferred_element_type=F32) * factor
        if masked:
            first = slot * key_rows + part * chunk
            pos = first + lax.broadcasted_iota(jnp.int32, (chunk, cols), 0)
            s = jnp.where(pos <= reach[...], s, LOW)
        return s

    def stats(slot, masked):
        @pl.loop(0, parts)
        def _(part):
            s = scores_of(slot, part, masked)
            here = jnp.maximum(jnp.max(s, axis=0, keepdims=True), FLOOR)
            e = jnp.exp2(s - here)
            if keep:
                ebuf[slot, rows_of(part), :] = e
                tops[slot * parts + part] = here
            old = top[...]
            new = jnp.maximum(old, here)
            total[...] = total[...] * jnp.exp2(old - new) + (
                jnp.sum(e, axis=0, keepdims=True) * jnp.exp2(here - new))
            top[...] = new

    def chip_stats(w, masked):
        @pl.loop(0, CORES)
        def _(b):
            slot = w * CORES + (core + b) % CORES

            @pl.when(b == 1)
            def _():
                arrived(kbuf, k_side, k_recv, slot)

            stats(slot, masked)

    def probs_of(slot, part, masked):
        if keep:
            return ebuf[slot, rows_of(part), :] * jnp.exp2(tops[slot * parts + part] - lse[...])
        return jnp.exp2(scores_of(slot, part, masked) - lse[...])

    def send_side(kind, w):
        sib_out[kind, w] = gpart[kind, w * CORES + (1 - core)].astype(BF16)
        grad_side(kind, w).start()

    def value_grads(w, masked):
        @pl.loop(0, CORES * parts)
        def _(i):
            slot = w * CORES + i // parts
            part = i % parts
            p = probs_of(slot, part, masked).astype(BF16)
            gpart[0, slot, rows_of(part), :] = jnp.dot(p, dorows[...], preferred_element_type=F32)

        send_side(0, w)

    def key_grads(w, masked):
        @pl.loop(0, CORES)
        def _(b):
            slot = w * CORES + (core + b) % CORES

            @pl.when(b == 1)
            def _():
                arrived(vbuf, v_side, v_recv, slot)

            @pl.loop(0, parts)
            def _(part):
                p = probs_of(slot, part, masked)
                dp = jnp.dot(vbuf[slot, rows_of(part), :], docols[...], preferred_element_type=F32)
                ds = (p * (dp - odot[...])).astype(BF16)
                gpart[1, slot, rows_of(part), :] = scale * jnp.dot(ds, qrows[...], preferred_element_type=F32)
                dqt[...] += jnp.dot(kbuf[slot, rows_of(part), :].T, ds, preferred_element_type=F32)

        send_side(1, w)

    def summed(kind, w):
        grad_side(kind, w).wait_recv()
        return gpart[kind, w * CORES + core] + sib_in[kind, w].astype(F32)

    def hand_down(kind, w):
        mine = gpart.at[kind, w * CORES + core]
        mine[...] = summed(kind, w)

        @pl.when(not_top)
        def _():
            grad_down(kind, w).wait_recv()
            mine[...] += ch_in[kind, w].astype(F32)

        ch_out[kind, w] = mine[...].astype(BF16)
        grad_down(kind, w).start()

    @pl.when(not_top)
    def _():
        @pl.loop(1, chip + 1)
        def _(s):
            from_below(kbuf, k_up, k_low, chip - s, True)
            across(kbuf, k_side, k_recv, chip - s).start()

        start_up(vbuf, v_up, v_low, chip)

    chip_stats(chip, True)

    @pl.loop(1, chip + 1)
    def _(s):
        w = chip - s

        @pl.when(is_top)
        def _():
            from_below(kbuf, k_up, k_low, w, False)
            across(kbuf, k_side, k_recv, w).start()

        chip_stats(w, False)

    @pl.when(not_top)
    def _():
        arrived(kbuf, k_side, k_recv, (chip + 1) * CORES + core)
        across(kbuf, k_side, k_recv, chip + 1).start()
        chip_stats(chip + 1, True)

    lse[...] = top[...] + jnp.log(total[...]) * math.log2(math.e)

    @pl.loop(0, chip)
    def _(t):
        w = chip - 1 - t
        value_grads(w, False)

        @pl.when(not_top)
        def _():
            from_below(vbuf, v_up, v_low, w, True)
            across(vbuf, v_side, v_recv, w).start()

        @pl.when(jnp.logical_and(is_top, t > 0))
        def _():
            hand_down(0, w + 1)

    @pl.when(jnp.logical_and(is_top, has_low))
    def _():
        hand_down(0, 0)

    @pl.loop(0, chip)
    def _(t):
        w = chip - 1 - t

        @pl.when(is_top)
        def _():
            from_below(vbuf, v_up, v_low, w, False)
            across(vbuf, v_side, v_recv, w).start()

        key_grads(w, False)

        hand_down(jnp.where(is_top, 1, 0), w)

    end = jnp.where(not_top, 2, 1)

    @pl.loop(0, end)
    def _(t):
        w = chip + end - 1 - t

        @pl.when(jnp.logical_and(not_top, w == chip))
        def _():
            @pl.loop(0, chip)
            def _(s):
                hand_down(1, chip - 1 - s)

        value_grads(w, True)

        @pl.when(w > chip)
        def _():
            arrived(vbuf, v_side, v_recv, w * CORES + core)
            across(vbuf, v_side, v_recv, w).start()

        key_grads(w, True)

        @pl.when(w > chip)
        def _():
            for kind in range(2):
                ch_out[kind, w] = summed(kind, w).astype(BF16)
                grad_up(kind).start()

    for h in range(heads):
        rows = slice(h * query_rows, (h + 1) * query_rows)
        dq_ref[:, h * HD:(h + 1) * HD] = (dqt[:, rows].T * scale).astype(BF16)

    for kind, out in ((0, dv_ref), (1, dk_ref)):
        gpart[kind, own_slot] = summed(kind, chip)

        @pl.when(has_low)
        def _():
            push(low_in.at[kind], low_in.at[kind], gl_send.at[kind], gl_recv.at[kind], side).wait_recv()
            gpart[kind, own_slot] = gpart[kind, own_slot] + low_in[kind].astype(F32)

        @pl.when(not_top)
        def _():
            grad_down(kind, chip).wait_recv()
            gpart[kind, own_slot] = gpart[kind, own_slot] + ch_in[kind, chip].astype(F32)

        out[...] = gpart[kind, own_slot].astype(BF16)

    for d in range(1, look + 1):
        @pl.when(me - d >= 0)
        def _():
            seg_copy(d, side).wait_send()

    @pl.when(has_low)
    def _():
        down(kbuf, k_down, k_recv).wait_send()
        down(vbuf, v_down, v_recv).wait_send()

    @pl.when(not_top)
    def _():
        for kind in range(2):
            grad_up(kind).wait_send()

    @pl.loop(0, chip + end)
    def _(w):
        across(kbuf, k_side, k_recv, w).wait_send()
        across(vbuf, v_side, v_recv, w).wait_send()
        for kind in range(2):
            grad_side(kind, w).wait_send()

        @pl.when(jnp.logical_and(not_top, w <= chip))
        def _():
            for half in range(HALVES):
                up(kbuf, k_up, k_low, w, half, side).wait_send()
                up(vbuf, v_up, v_low, w, half, side).wait_send()

        @pl.when(w < chip)
        def _():
            for kind in range(2):
                grad_down(kind, w).wait_send()


def pass_on(a_ref, b_ref, c_ref, a_out, b_out, c_out):
    a_out[...] = a_ref[...]
    b_out[...] = b_ref[...]
    c_out[...] = c_ref[...]


def per_device(queries, keys, values, grad_out, saved_out, segment_ids, frame_flags):
    ranks = lax.axis_size("ctx")
    chips = ranks // CORES
    key_rows = keys.shape[1]
    query_rows, width = queries.shape[1:]
    cols = query_rows * (width // HD)
    look = (SEG_MOST + key_rows - 2) // key_rows
    assert look <= CORES and ranks % CORES == 0
    chunk = math.gcd(key_rows, 512)
    parts = key_rows // chunk
    keep = ranks * key_rows * cols * 4 <= KEEP_BYTES
    kept = ranks if keep else 1
    dma = pltpu.SemaphoreType.DMA
    block = (key_rows, HD)
    grads = (2, chips) + block
    vmem = pl.BlockSpec(memory_space=pltpu.VMEM)
    grad_queries, grad_keys, grad_values = pl.pallas_call(
        functools.partial(fused, ranks, look, chunk, keep),
        out_shape=(
            jax.ShapeDtypeStruct((query_rows, width), BF16),
            jax.ShapeDtypeStruct(block, BF16),
            jax.ShapeDtypeStruct(block, BF16),
        ),
        in_specs=[vmem] * 7,
        out_specs=(vmem,) * 3,
        scratch_shapes=[
            pltpu.VMEM((ranks,) + block, BF16),
            pltpu.VMEM((ranks,) + block, BF16),
            pltpu.VMEM((kept, key_rows, cols), F32) if keep else pltpu.VMEM((8, 128), F32),
            pltpu.VMEM((kept * parts, 1, cols), F32),
            pltpu.VMEM((HD, cols), BF16),
            pltpu.VMEM((cols, HD), BF16),
            pltpu.VMEM((HD, cols), BF16),
            pltpu.VMEM((cols, HD), BF16),
            pltpu.VMEM((1, cols), jnp.int32),
            pltpu.VMEM((1, cols), F32),
            pltpu.VMEM((1, cols), F32),
            pltpu.VMEM((1, cols), F32),
            pltpu.VMEM((1, cols), F32),
            pltpu.VMEM((HD, cols), F32),
            pltpu.VMEM((2, ranks) + block, F32),
            pltpu.VMEM(grads, BF16),
            pltpu.VMEM(grads, BF16),
            pltpu.VMEM(grads, BF16),
            pltpu.VMEM(grads, BF16),
            pltpu.VMEM((2,) + block, BF16),
            pltpu.VMEM((look, 1, key_rows), jnp.int32),
            dma((chips, HALVES)), dma((chips, HALVES)), dma((chips,)), dma((1,)), dma((ranks,)),
            dma((chips, HALVES)), dma((chips, HALVES)), dma((chips,)), dma((1,)), dma((ranks,)),
            dma((2, chips)), dma((2, chips)), dma((2, chips)), dma((2, chips)),
            dma((2,)), dma((2,)), dma((look,)), dma((look,)),
        ],
        compiler_params=pltpu.CompilerParams(
            collective_id=0, has_side_effects=True, vmem_limit_bytes=60 * 1024 * 1024
        ),
        cost_estimate=pl.CostEstimate(
            flops=12 * cols * ranks * key_rows * HD,
            bytes_accessed=8 * cols * HD,
            transcendentals=cols * ranks * key_rows,
        ),
    )(queries[0], keys[0], values[0], grad_out[0], saved_out[0], segment_ids, frame_flags)
    results = pl.pallas_call(
        pass_on,
        out_shape=tuple(jax.ShapeDtypeStruct(r.shape, r.dtype) for r in (grad_queries, grad_keys, grad_values)),
        in_specs=[vmem] * 3,
        out_specs=(vmem,) * 3,
    )(grad_queries, grad_keys, grad_values)
    return tuple(r[None] for r in results)


def solution(mesh):
    return jax.shard_map(
        per_device,
        mesh=mesh,
        in_specs=(
            P("dp", "ctx", None),
            P("dp", "ctx", None),
            P("dp", "ctx", None),
            P("dp", "ctx", None),
            P("dp", "ctx", None),
            P("dp", "ctx"),
            P("dp", None),
        ),
        out_specs=(P("dp", "ctx", None), P("dp", "ctx", None), P("dp", "ctx", None)),
        check_vma=False,
    )
```

```python
import functools
import math

import jax
import jax.numpy as jnp
from jax import lax
from jax.experimental import pallas as pl
from jax.experimental.pallas import tpu as pltpu
from jax.sharding import PartitionSpec as P

HD = 128
SEG_MOST = 1024
CORES = 2
HALVES = 2
LOW = -1e30
FLOOR = -1e29
KEEP_BYTES = 20 * 1024 * 1024
F32 = jnp.float32
BF16 = jnp.bfloat16


def push(src, dst, send, recv, rank):
    return pltpu.make_async_remote_copy(
        src_ref=src,
        dst_ref=dst,
        send_sem=send,
        recv_sem=recv,
        device_id={"ctx": rank},
        device_id_type=pl.DeviceIdType.MESH,
    )


def fused(
    ranks, look, chunk, keep,
    q_ref, k_ref, v_ref, do_ref, o_ref, seg_ref, flag_ref,
    dq_ref, dk_ref, dv_ref,
    kbuf, vbuf, ebuf, tops, qcols, qrows, docols, dorows, reach, odot, top, total, lse, dqt,
    gpart, sib_out, sib_in, ch_out, ch_in, low_in, segs,
    k_up, k_low, k_side, k_down, k_recv, v_up, v_low, v_side, v_down, v_recv,
    gs_send, gs_recv, gc_send, gc_recv, gl_send, gl_recv, seg_send, seg_recv,
):
    chips = ranks // CORES
    key_rows = k_ref.shape[0]
    query_rows = q_ref.shape[0]
    heads = q_ref.shape[1] // HD
    cols = query_rows * heads
    parts = key_rows // chunk
    scale = 1.0 / math.sqrt(HD)
    factor = scale * math.log2(math.e)
    me = lax.axis_index("ctx")
    chip = me // CORES
    core = me % CORES
    side = chip * CORES + (1 - core)
    is_top = chip == chips - 1
    not_top = chip < chips - 1
    has_low = chip > 0
    own_slot = me
    reach_ranks = max(look, CORES)

    barrier = pltpu.get_barrier_semaphore()
    there = jnp.int32(0)
    for d in range(1, reach_ranks + 1):
        @pl.when(me + d < ranks)
        def _():
            pl.semaphore_signal(barrier, inc=1, device_id={"ctx": me + d},
                                device_id_type=pl.DeviceIdType.MESH)

        @pl.when(me - d >= 0)
        def _():
            pl.semaphore_signal(barrier, inc=1, device_id={"ctx": me - d},
                                device_id_type=pl.DeviceIdType.MESH)

        there = there + jnp.where(me + d < ranks, 1, 0) + jnp.where(me - d >= 0, 1, 0)
    kbuf[own_slot] = k_ref[...]
    vbuf[own_slot] = v_ref[...]
    pl.semaphore_wait(barrier, there)

    def up(buf, sems, recv, w, half, rank):
        rows = pl.ds(half * (key_rows // HALVES), key_rows // HALVES)
        place = buf.at[w * CORES + core, rows]
        return push(place, place, sems.at[w, half], recv.at[w, half], rank)

    def start_up(buf, sems, recv, w):
        for half in range(HALVES):
            up(buf, sems, recv, w, half, me + CORES).start()

    def from_below(buf, sems, recv, w, forward):
        for half in range(HALVES):
            up(buf, sems, recv, w, half, side).wait_recv()
            if forward:
                up(buf, sems, recv, w, half, me + CORES).start()

    def across(buf, sems, recv, w):
        slot = w * CORES + core
        return push(buf.at[slot], buf.at[slot], sems.at[w], recv.at[slot], side)

    def down(buf, sems, recv):
        return push(buf.at[own_slot], buf.at[own_slot], sems.at[0], recv.at[own_slot], me - CORES)

    def arrived(buf, sems, recv, slot):
        push(buf.at[slot], buf.at[slot], sems.at[0], recv.at[slot], side).wait_recv()

    def seg_copy(d, rank):
        return push(seg_ref, segs.at[d - 1], seg_send.at[d - 1], seg_recv.at[d - 1], rank)

    def grad_side(kind, w):
        return push(sib_out.at[kind, w], sib_in.at[kind, w], gs_send.at[kind, w], gs_recv.at[kind, w], side)

    def grad_down(kind, w):
        return push(ch_out.at[kind, w], ch_in.at[kind, w], gc_send.at[kind, w], gc_recv.at[kind, w], me - CORES)

    def grad_up(kind):
        return push(ch_out.at[kind, chip + 1], low_in.at[kind], gl_send.at[kind], gl_recv.at[kind], me + CORES)

    @pl.when(not_top)
    def _():
        start_up(kbuf, k_up, k_low, chip)

    across(kbuf, k_side, k_recv, chip).start()
    for d in range(1, look + 1):
        @pl.when(me - d >= 0)
        def _():
            seg_copy(d, me - d).start()

    @pl.when(has_low)
    def _():
        down(kbuf, k_down, k_recv).start()
        down(vbuf, v_down, v_recv).start()

    across(vbuf, v_side, v_recv, chip).start()

    for h in range(heads):
        at = slice(h * HD, (h + 1) * HD)
        rows = slice(h * query_rows, (h + 1) * query_rows)
        q_h = q_ref[:, at]
        do_h = do_ref[:, at]
        qrows[rows, :] = q_h
        dorows[rows, :] = do_h
        qcols[:, rows] = q_h.T
        docols[:, rows] = do_h.T
        odot[:, rows] = jnp.sum((do_h.astype(F32) * o_ref[:, at].astype(F32)).T, axis=0, keepdims=True)
    top[...] = jnp.full(top.shape, FLOOR, F32)
    total[...] = jnp.zeros(total.shape, F32)
    dqt[...] = jnp.zeros(dqt.shape, F32)

    for d in range(1, look + 1):
        @pl.when(me + d < ranks)
        def _():
            seg_copy(d, side).wait_recv()

        @pl.when(me + d >= ranks)
        def _():
            segs[d - 1] = jnp.full(seg_ref.shape, 1 << 20, jnp.int32)

    seg_q = seg_ref[:, key_rows - query_rows:].astype(F32)
    seg_col = jnp.broadcast_to(seg_q, (HD, query_rows)).T
    counts = jnp.zeros((query_rows, HD), F32)
    for d in range(look + 1):
        for j in range(key_rows // HD):
            at = slice(j * HD, (j + 1) * HD)
            piece = (seg_ref[:, at] if d == 0 else segs[d - 1, :, at]).astype(F32)
            counts = counts + jnp.where(piece <= seg_col, 1.0, 0.0)
    count = jnp.sum(counts, axis=1, keepdims=True)
    segments = flag_ref.shape[1]
    ids = lax.broadcasted_iota(jnp.int32, (query_rows, segments), 1).astype(F32)
    flags = jnp.broadcast_to(flag_ref[...].astype(F32), (query_rows, segments))
    framed = jnp.sum(jnp.where(ids == seg_col[:, :1], flags, 0.0), axis=1, keepdims=True)
    local = (key_rows - query_rows) + lax.broadcasted_iota(jnp.int32, (query_rows, 1), 0).astype(F32)
    last = jnp.where(framed == 1.0, count - 1.0, local)
    last_row = jnp.broadcast_to(last, (query_rows, HD)).T[:1, :].astype(jnp.int32) + me * key_rows
    for h in range(heads):
        reach[:, h * query_rows:(h + 1) * query_rows] = last_row

    def rows_of(part):
        return pl.ds(pl.multiple_of(part * chunk, chunk), chunk)

    def scores_of(slot, part, masked):
        s = jnp.dot(kbuf[slot, rows_of(part), :], qcols[...], preferred_element_type=F32) * factor
        if masked:
            first = slot * key_rows + part * chunk
            pos = lax.broadcasted_iota(jnp.int32, (chunk, cols), 0)
            s = jnp.where(pos <= reach[...] - first, s, LOW)
        return s

    def stats(slot, masked):
        @pl.loop(0, parts)
        def _(part):
            s = scores_of(slot, part, masked)
            here = jnp.maximum(jnp.max(s, axis=0, keepdims=True), FLOOR)
            e = jnp.exp2(s - here)
            if keep:
                ebuf[slot, rows_of(part), :] = e.astype(BF16)
                tops[slot * parts + part] = here
            old = top[...]
            new = jnp.maximum(old, here)
            total[...] = total[...] * jnp.exp2(old - new) + (
                jnp.sum(e, axis=0, keepdims=True) * jnp.exp2(here - new))
            top[...] = new

    def chip_stats(w, masked):
        @pl.loop(0, CORES)
        def _(b):
            slot = w * CORES + (core + b) % CORES

            @pl.when(b == 1)
            def _():
                arrived(kbuf, k_side, k_recv, slot)

            stats(slot, masked)

    def probs_of(slot, part, masked):
        if keep:
            level = jnp.exp2(tops[slot * parts + part] - lse[...])
            return ebuf[slot, rows_of(part), :].astype(F32) * level
        return jnp.exp2(scores_of(slot, part, masked) - lse[...])

    def send_side(kind, w):
        sib_out[kind, w] = gpart[kind, w * CORES + (1 - core)].astype(BF16)
        grad_side(kind, w).start()

    def value_grads(w, masked):
        @pl.loop(0, CORES * parts)
        def _(i):
            slot = w * CORES + i // parts
            part = i % parts
            p = probs_of(slot, part, masked).astype(BF16)
            if keep:
                ebuf[slot, rows_of(part), :] = p
            gpart[0, slot, rows_of(part), :] = jnp.dot(p, dorows[...], preferred_element_type=F32)

        send_side(0, w)

    def key_grads(w, masked):
        @pl.loop(0, CORES)
        def _(b):
            slot = w * CORES + (core + b) % CORES

            @pl.when(b == 1)
            def _():
                arrived(vbuf, v_side, v_recv, slot)

            @pl.loop(0, parts)
            def _(part):
                p = ebuf[slot, rows_of(part), :].astype(F32) if keep else probs_of(slot, part, masked)
                dp = jnp.dot(vbuf[slot, rows_of(part), :], docols[...], preferred_element_type=F32)
                ds = (p * (dp - odot[...])).astype(BF16)
                gpart[1, slot, rows_of(part), :] = scale * jnp.dot(ds, qrows[...], preferred_element_type=F32)
                dqt[...] += jnp.dot(kbuf[slot, rows_of(part), :].T, ds, preferred_element_type=F32)

        send_side(1, w)

    def summed(kind, w):
        grad_side(kind, w).wait_recv()
        return gpart[kind, w * CORES + core] + sib_in[kind, w].astype(F32)

    def hand_down(kind, w):
        mine = gpart.at[kind, w * CORES + core]
        mine[...] = summed(kind, w)

        @pl.when(not_top)
        def _():
            grad_down(kind, w).wait_recv()
            mine[...] += ch_in[kind, w].astype(F32)

        ch_out[kind, w] = mine[...].astype(BF16)
        grad_down(kind, w).start()

    @pl.when(not_top)
    def _():
        @pl.loop(1, chip + 1)
        def _(s):
            from_below(kbuf, k_up, k_low, chip - s, True)
            across(kbuf, k_side, k_recv, chip - s).start()

        start_up(vbuf, v_up, v_low, chip)

    chip_stats(chip, True)

    @pl.loop(1, chip + 1)
    def _(s):
        w = chip - s

        @pl.when(is_top)
        def _():
            from_below(kbuf, k_up, k_low, w, False)
            across(kbuf, k_side, k_recv, w).start()

        chip_stats(w, False)

    @pl.when(not_top)
    def _():
        arrived(kbuf, k_side, k_recv, (chip + 1) * CORES + core)
        across(kbuf, k_side, k_recv, chip + 1).start()
        chip_stats(chip + 1, True)

    lse[...] = top[...] + jnp.log(total[...]) * math.log2(math.e)

    @pl.loop(0, chip)
    def _(t):
        w = chip - 1 - t
        value_grads(w, False)

        @pl.when(not_top)
        def _():
            from_below(vbuf, v_up, v_low, w, True)
            across(vbuf, v_side, v_recv, w).start()

        @pl.when(jnp.logical_and(is_top, t > 0))
        def _():
            hand_down(0, w + 1)

    @pl.when(jnp.logical_and(is_top, has_low))
    def _():
        hand_down(0, 0)

    @pl.loop(0, chip)
    def _(t):
        w = chip - 1 - t

        @pl.when(is_top)
        def _():
            from_below(vbuf, v_up, v_low, w, False)
            across(vbuf, v_side, v_recv, w).start()

        key_grads(w, False)

        hand_down(jnp.where(is_top, 1, 0), w)

    end = jnp.where(not_top, 2, 1)

    @pl.loop(0, end)
    def _(t):
        w = chip + end - 1 - t

        @pl.when(jnp.logical_and(not_top, w == chip))
        def _():
            @pl.loop(0, chip)
            def _(s):
                hand_down(1, chip - 1 - s)

        value_grads(w, True)

        @pl.when(w > chip)
        def _():
            arrived(vbuf, v_side, v_recv, w * CORES + core)
            across(vbuf, v_side, v_recv, w).start()

        key_grads(w, True)

        @pl.when(w > chip)
        def _():
            for kind in range(2):
                ch_out[kind, w] = summed(kind, w).astype(BF16)
                grad_up(kind).start()

    for h in range(heads):
        rows = slice(h * query_rows, (h + 1) * query_rows)
        dq_ref[:, h * HD:(h + 1) * HD] = (dqt[:, rows].T * scale).astype(BF16)

    for kind, out in ((0, dv_ref), (1, dk_ref)):
        gpart[kind, own_slot] = summed(kind, chip)

        @pl.when(has_low)
        def _():
            push(low_in.at[kind], low_in.at[kind], gl_send.at[kind], gl_recv.at[kind], side).wait_recv()
            gpart[kind, own_slot] = gpart[kind, own_slot] + low_in[kind].astype(F32)

        @pl.when(not_top)
        def _():
            grad_down(kind, chip).wait_recv()
            gpart[kind, own_slot] = gpart[kind, own_slot] + ch_in[kind, chip].astype(F32)

        out[...] = gpart[kind, own_slot].astype(BF16)

    for d in range(1, look + 1):
        @pl.when(me - d >= 0)
        def _():
            seg_copy(d, side).wait_send()

    @pl.when(has_low)
    def _():
        down(kbuf, k_down, k_recv).wait_send()
        down(vbuf, v_down, v_recv).wait_send()

    @pl.when(not_top)
    def _():
        for kind in range(2):
            grad_up(kind).wait_send()

    @pl.loop(0, chip + end)
    def _(w):
        across(kbuf, k_side, k_recv, w).wait_send()
        across(vbuf, v_side, v_recv, w).wait_send()
        for kind in range(2):
            grad_side(kind, w).wait_send()

        @pl.when(jnp.logical_and(not_top, w <= chip))
        def _():
            for half in range(HALVES):
                up(kbuf, k_up, k_low, w, half, side).wait_send()
                up(vbuf, v_up, v_low, w, half, side).wait_send()

        @pl.when(w < chip)
        def _():
            for kind in range(2):
                grad_down(kind, w).wait_send()


def pass_on(a_ref, b_ref, c_ref, a_out, b_out, c_out, sems):
    pairs = ((a_ref, a_out), (b_ref, b_out), (c_ref, c_out))
    copies = [pltpu.make_async_copy(src, dst, sems.at[i]) for i, (src, dst) in enumerate(pairs)]
    for copy in copies:
        copy.start()
    for copy in copies:
        copy.wait()


def per_device(queries, keys, values, grad_out, saved_out, segment_ids, frame_flags):
    ranks = lax.axis_size("ctx")
    chips = ranks // CORES
    key_rows = keys.shape[1]
    query_rows, width = queries.shape[1:]
    cols = query_rows * (width // HD)
    look = (SEG_MOST + key_rows - 2) // key_rows
    assert look <= CORES and ranks % CORES == 0
    chunk = math.gcd(key_rows, 512)
    parts = key_rows // chunk
    keep = ranks * key_rows * cols * 4 <= KEEP_BYTES
    kept = ranks if keep else 1
    dma = pltpu.SemaphoreType.DMA
    block = (key_rows, HD)
    grads = (2, chips) + block
    vmem = pl.BlockSpec(memory_space=pltpu.VMEM)
    grad_queries, grad_keys, grad_values = pl.pallas_call(
        functools.partial(fused, ranks, look, chunk, keep),
        out_shape=(
            jax.ShapeDtypeStruct((query_rows, width), BF16),
            jax.ShapeDtypeStruct(block, BF16),
            jax.ShapeDtypeStruct(block, BF16),
        ),
        in_specs=[vmem] * 7,
        out_specs=(vmem,) * 3,
        scratch_shapes=[
            pltpu.VMEM((ranks,) + block, BF16),
            pltpu.VMEM((ranks,) + block, BF16),
            pltpu.VMEM((kept, key_rows, cols), BF16) if keep else pltpu.VMEM((8, 128), F32),
            pltpu.VMEM((kept * parts, 1, cols), F32),
            pltpu.VMEM((HD, cols), BF16),
            pltpu.VMEM((cols, HD), BF16),
            pltpu.VMEM((HD, cols), BF16),
            pltpu.VMEM((cols, HD), BF16),
            pltpu.VMEM((1, cols), jnp.int32),
            pltpu.VMEM((1, cols), F32),
            pltpu.VMEM((1, cols), F32),
            pltpu.VMEM((1, cols), F32),
            pltpu.VMEM((1, cols), F32),
            pltpu.VMEM((HD, cols), F32),
            pltpu.VMEM((2, ranks) + block, F32),
            pltpu.VMEM(grads, BF16),
            pltpu.VMEM(grads, BF16),
            pltpu.VMEM(grads, BF16),
            pltpu.VMEM(grads, BF16),
            pltpu.VMEM((2,) + block, BF16),
            pltpu.VMEM((look, 1, key_rows), jnp.int32),
            dma((chips, HALVES)), dma((chips, HALVES)), dma((chips,)), dma((1,)), dma((ranks,)),
            dma((chips, HALVES)), dma((chips, HALVES)), dma((chips,)), dma((1,)), dma((ranks,)),
            dma((2, chips)), dma((2, chips)), dma((2, chips)), dma((2, chips)),
            dma((2,)), dma((2,)), dma((look,)), dma((look,)),
        ],
        compiler_params=pltpu.CompilerParams(
            collective_id=0, has_side_effects=True, vmem_limit_bytes=60 * 1024 * 1024
        ),
        cost_estimate=pl.CostEstimate(
            flops=12 * cols * ranks * key_rows * HD,
            bytes_accessed=8 * cols * HD,
            transcendentals=cols * ranks * key_rows,
        ),
    )(queries[0], keys[0], values[0], grad_out[0], saved_out[0], segment_ids, frame_flags)
    results = pl.pallas_call(
        pass_on,
        out_shape=tuple(jax.ShapeDtypeStruct(r.shape, r.dtype) for r in (grad_queries, grad_keys, grad_values)),
        in_specs=[pl.BlockSpec(memory_space=pl.ANY)] * 3,
        out_specs=(pl.BlockSpec(memory_space=pl.ANY),) * 3,
        scratch_shapes=[dma((3,))],
    )(grad_queries, grad_keys, grad_values)
    return tuple(r[None] for r in results)


def solution(mesh):
    return jax.shard_map(
        per_device,
        mesh=mesh,
        in_specs=(
            P("dp", "ctx", None),
            P("dp", "ctx", None),
            P("dp", "ctx", None),
            P("dp", "ctx", None),
            P("dp", "ctx", None),
            P("dp", "ctx"),
            P("dp", None),
        ),
        out_specs=(P("dp", "ctx", None), P("dp", "ctx", None), P("dp", "ctx", None)),
        check_vma=False,
    )
```

```python
import functools
import math

import jax
import jax.numpy as jnp
from jax import lax
from jax.experimental import pallas as pl
from jax.experimental.pallas import tpu as pltpu
from jax.sharding import PartitionSpec as P

HD = 128
SEG_MOST = 1024
CORES = 2
HALVES = 2
LOW = -1e30
FLOOR = -1e29
KEEP_BYTES = 20 * 1024 * 1024
F32 = jnp.float32
BF16 = jnp.bfloat16


def push(src, dst, send, recv, rank):
    return pltpu.make_async_remote_copy(
        src_ref=src,
        dst_ref=dst,
        send_sem=send,
        recv_sem=recv,
        device_id={"ctx": rank},
        device_id_type=pl.DeviceIdType.MESH,
    )


def fused(
    ranks, look, chunk, keep,
    q_ref, k_ref, v_ref, do_ref, o_ref, seg_ref, flag_ref,
    dq_ref, dk_ref, dv_ref,
    kbuf, vbuf, ebuf, tops, qcols, qrows, docols, dorows, reach, odot, top, total, lse, dqt,
    gpart, sib_out, sib_in, ch_out, ch_in, low_in, segs,
    k_up, k_low, k_side, k_down, k_recv, v_up, v_low, v_side, v_down, v_recv,
    gs_send, gs_recv, gc_send, gc_recv, gl_send, gl_recv, seg_send, seg_recv,
):
    chips = ranks // CORES
    key_rows = k_ref.shape[0]
    query_rows = q_ref.shape[0]
    heads = q_ref.shape[1] // HD
    cols = query_rows * heads
    parts = key_rows // chunk
    scale = 1.0 / math.sqrt(HD)
    factor = scale * math.log2(math.e)
    me = lax.axis_index("ctx")
    chip = me // CORES
    core = me % CORES
    side = chip * CORES + (1 - core)
    is_top = chip == chips - 1
    not_top = chip < chips - 1
    has_low = chip > 0
    own_slot = me
    reach_ranks = max(look, CORES)

    barrier = pltpu.get_barrier_semaphore()
    there = jnp.int32(0)
    for d in range(1, reach_ranks + 1):
        @pl.when(me + d < ranks)
        def _():
            pl.semaphore_signal(barrier, inc=1, device_id={"ctx": me + d},
                                device_id_type=pl.DeviceIdType.MESH)

        @pl.when(me - d >= 0)
        def _():
            pl.semaphore_signal(barrier, inc=1, device_id={"ctx": me - d},
                                device_id_type=pl.DeviceIdType.MESH)

        there = there + jnp.where(me + d < ranks, 1, 0) + jnp.where(me - d >= 0, 1, 0)
    kbuf[own_slot] = k_ref[...]
    vbuf[own_slot] = v_ref[...]
    pl.semaphore_wait(barrier, there)

    def up(buf, sems, recv, w, half, rank):
        rows = pl.ds(half * (key_rows // HALVES), key_rows // HALVES)
        place = buf.at[w * CORES + core, rows]
        return push(place, place, sems.at[w, half], recv.at[w, half], rank)

    def start_up(buf, sems, recv, w):
        for half in range(HALVES):
            up(buf, sems, recv, w, half, me + CORES).start()

    def from_below(buf, sems, recv, w, forward):
        for half in range(HALVES):
            up(buf, sems, recv, w, half, side).wait_recv()
            if forward:
                up(buf, sems, recv, w, half, me + CORES).start()

    def across(buf, sems, recv, w):
        slot = w * CORES + core
        return push(buf.at[slot], buf.at[slot], sems.at[w], recv.at[slot], side)

    def down(buf, sems, recv):
        return push(buf.at[own_slot], buf.at[own_slot], sems.at[0], recv.at[own_slot], me - CORES)

    def arrived(buf, sems, recv, slot):
        push(buf.at[slot], buf.at[slot], sems.at[0], recv.at[slot], side).wait_recv()

    def seg_copy(d, rank):
        return push(seg_ref, segs.at[d - 1], seg_send.at[d - 1], seg_recv.at[d - 1], rank)

    def grad_side(kind, w):
        return push(sib_out.at[kind, w], sib_in.at[kind, w], gs_send.at[kind, w], gs_recv.at[kind, w], side)

    def half_of(half):
        return pl.ds(half * (key_rows // HALVES), key_rows // HALVES)

    def grad_down(kind, w, half, rank):
        rows = half_of(half)
        return push(ch_out.at[kind, w, rows], ch_in.at[kind, w, rows],
                    gc_send.at[kind, w, half], gc_recv.at[kind, w, half], rank)

    def grad_up(kind):
        return push(ch_out.at[kind, chip + 1], low_in.at[kind], gl_send.at[kind], gl_recv.at[kind], me + CORES)

    @pl.when(not_top)
    def _():
        start_up(kbuf, k_up, k_low, chip)

    across(kbuf, k_side, k_recv, chip).start()
    for d in range(1, look + 1):
        @pl.when(me - d >= 0)
        def _():
            seg_copy(d, me - d).start()

    @pl.when(has_low)
    def _():
        down(kbuf, k_down, k_recv).start()
        down(vbuf, v_down, v_recv).start()

    across(vbuf, v_side, v_recv, chip).start()

    for h in range(heads):
        at = slice(h * HD, (h + 1) * HD)
        rows = slice(h * query_rows, (h + 1) * query_rows)
        q_h = q_ref[:, at]
        do_h = do_ref[:, at]
        qrows[rows, :] = q_h
        dorows[rows, :] = do_h
        qcols[:, rows] = q_h.T
        docols[:, rows] = do_h.T
        odot[:, rows] = jnp.sum((do_h.astype(F32) * o_ref[:, at].astype(F32)).T, axis=0, keepdims=True)
    top[...] = jnp.full(top.shape, FLOOR, F32)
    total[...] = jnp.zeros(total.shape, F32)
    dqt[...] = jnp.zeros(dqt.shape, F32)

    for d in range(1, look + 1):
        @pl.when(me + d < ranks)
        def _():
            seg_copy(d, side).wait_recv()

        @pl.when(me + d >= ranks)
        def _():
            segs[d - 1] = jnp.full(seg_ref.shape, 1 << 20, jnp.int32)

    seg_q = seg_ref[:, key_rows - query_rows:].astype(F32)
    seg_col = jnp.broadcast_to(seg_q, (HD, query_rows)).T
    counts = jnp.zeros((query_rows, HD), F32)
    for d in range(look + 1):
        for j in range(key_rows // HD):
            at = slice(j * HD, (j + 1) * HD)
            piece = (seg_ref[:, at] if d == 0 else segs[d - 1, :, at]).astype(F32)
            counts = counts + jnp.where(piece <= seg_col, 1.0, 0.0)
    count = jnp.sum(counts, axis=1, keepdims=True)
    segments = flag_ref.shape[1]
    ids = lax.broadcasted_iota(jnp.int32, (query_rows, segments), 1).astype(F32)
    flags = jnp.broadcast_to(flag_ref[...].astype(F32), (query_rows, segments))
    framed = jnp.sum(jnp.where(ids == seg_col[:, :1], flags, 0.0), axis=1, keepdims=True)
    local = (key_rows - query_rows) + lax.broadcasted_iota(jnp.int32, (query_rows, 1), 0).astype(F32)
    last = jnp.where(framed == 1.0, count - 1.0, local)
    last_row = jnp.broadcast_to(last, (query_rows, HD)).T[:1, :].astype(jnp.int32) + me * key_rows
    for h in range(heads):
        reach[:, h * query_rows:(h + 1) * query_rows] = last_row

    def rows_of(part):
        return pl.ds(pl.multiple_of(part * chunk, chunk), chunk)

    def scores_of(slot, part, masked):
        s = jnp.dot(kbuf[slot, rows_of(part), :], qcols[...], preferred_element_type=F32) * factor
        if masked:
            first = slot * key_rows + part * chunk
            pos = first + lax.broadcasted_iota(jnp.int32, (chunk, cols), 0)
            s = jnp.where(pos <= reach[...], s, LOW)
        return s

    def stats(slot, masked):
        @pl.loop(0, parts)
        def _(part):
            s = scores_of(slot, part, masked)
            here = jnp.maximum(jnp.max(s, axis=0, keepdims=True), FLOOR)
            e = jnp.exp2(s - here)
            if keep:
                ebuf[slot, rows_of(part), :] = e
                tops[slot * parts + part] = here
            old = top[...]
            new = jnp.maximum(old, here)
            total[...] = total[...] * jnp.exp2(old - new) + (
                jnp.sum(e, axis=0, keepdims=True) * jnp.exp2(here - new))
            top[...] = new

    def chip_stats(w, masked):
        @pl.loop(0, CORES)
        def _(b):
            slot = w * CORES + (core + b) % CORES

            @pl.when(b == 1)
            def _():
                arrived(kbuf, k_side, k_recv, slot)

            stats(slot, masked)

    def probs_of(slot, part, masked):
        if keep:
            return ebuf[slot, rows_of(part), :] * jnp.exp2(tops[slot * parts + part] - lse[...])
        return jnp.exp2(scores_of(slot, part, masked) - lse[...])

    def send_side(kind, w):
        sib_out[kind, w] = gpart[kind, w * CORES + (1 - core)].astype(BF16)
        grad_side(kind, w).start()

    def value_grads(w, masked):
        @pl.loop(0, CORES * parts)
        def _(i):
            slot = w * CORES + i // parts
            part = i % parts
            p = probs_of(slot, part, masked).astype(BF16)
            gpart[0, slot, rows_of(part), :] = jnp.dot(p, dorows[...], preferred_element_type=F32)

        send_side(0, w)

    def key_grads(w, masked):
        @pl.loop(0, CORES)
        def _(b):
            slot = w * CORES + (core + b) % CORES

            @pl.when(b == 1)
            def _():
                arrived(vbuf, v_side, v_recv, slot)

            @pl.loop(0, parts)
            def _(part):
                p = probs_of(slot, part, masked)
                dp = jnp.dot(vbuf[slot, rows_of(part), :], docols[...], preferred_element_type=F32)
                ds = (p * (dp - odot[...])).astype(BF16)
                gpart[1, slot, rows_of(part), :] = scale * jnp.dot(ds, qrows[...], preferred_element_type=F32)
                dqt[...] += jnp.dot(kbuf[slot, rows_of(part), :].T, ds, preferred_element_type=F32)

        send_side(1, w)

    def summed(kind, w):
        grad_side(kind, w).wait_recv()
        return gpart[kind, w * CORES + core] + sib_in[kind, w].astype(F32)

    def hand_down(kind, w):
        mine = gpart.at[kind, w * CORES + core]
        mine[...] = summed(kind, w)
        for half in range(HALVES):
            rows = half_of(half)

            @pl.when(not_top)
            def _():
                grad_down(kind, w, half, side).wait_recv()
                mine[rows, :] += ch_in[kind, w, rows, :].astype(F32)

            ch_out[kind, w, rows, :] = mine[rows, :].astype(BF16)
            grad_down(kind, w, half, me - CORES).start()

    @pl.when(not_top)
    def _():
        @pl.loop(1, chip + 1)
        def _(s):
            from_below(kbuf, k_up, k_low, chip - s, True)
            across(kbuf, k_side, k_recv, chip - s).start()

        start_up(vbuf, v_up, v_low, chip)

    chip_stats(chip, True)

    @pl.loop(1, chip + 1)
    def _(s):
        w = chip - s

        @pl.when(is_top)
        def _():
            from_below(kbuf, k_up, k_low, w, False)
            across(kbuf, k_side, k_recv, w).start()

        chip_stats(w, False)

    @pl.when(not_top)
    def _():
        arrived(kbuf, k_side, k_recv, (chip + 1) * CORES + core)
        across(kbuf, k_side, k_recv, chip + 1).start()
        chip_stats(chip + 1, True)

    lse[...] = top[...] + jnp.log(total[...]) * math.log2(math.e)

    @pl.loop(0, chip)
    def _(t):
        w = chip - 1 - t
        value_grads(w, False)

        @pl.when(not_top)
        def _():
            from_below(vbuf, v_up, v_low, w, True)
            across(vbuf, v_side, v_recv, w).start()

        @pl.when(jnp.logical_and(is_top, t > 0))
        def _():
            hand_down(0, w + 1)

    @pl.when(jnp.logical_and(is_top, has_low))
    def _():
        hand_down(0, 0)

    @pl.loop(0, chip)
    def _(t):
        w = chip - 1 - t

        @pl.when(is_top)
        def _():
            from_below(vbuf, v_up, v_low, w, False)
            across(vbuf, v_side, v_recv, w).start()

        key_grads(w, False)

        hand_down(jnp.where(is_top, 1, 0), w)

    end = jnp.where(not_top, 2, 1)

    @pl.loop(0, end)
    def _(t):
        w = chip + end - 1 - t

        @pl.when(jnp.logical_and(not_top, w == chip))
        def _():
            @pl.loop(0, chip)
            def _(s):
                hand_down(1, chip - 1 - s)

        value_grads(w, True)

        @pl.when(w > chip)
        def _():
            arrived(vbuf, v_side, v_recv, w * CORES + core)
            across(vbuf, v_side, v_recv, w).start()

        key_grads(w, True)

        @pl.when(w > chip)
        def _():
            for kind in range(2):
                ch_out[kind, w] = summed(kind, w).astype(BF16)
                grad_up(kind).start()

    for h in range(heads):
        rows = slice(h * query_rows, (h + 1) * query_rows)
        dq_ref[:, h * HD:(h + 1) * HD] = (dqt[:, rows].T * scale).astype(BF16)

    for kind, out in ((0, dv_ref), (1, dk_ref)):
        gpart[kind, own_slot] = summed(kind, chip)

        @pl.when(has_low)
        def _():
            push(low_in.at[kind], low_in.at[kind], gl_send.at[kind], gl_recv.at[kind], side).wait_recv()
            gpart[kind, own_slot] = gpart[kind, own_slot] + low_in[kind].astype(F32)

        @pl.when(not_top)
        def _():
            for half in range(HALVES):
                grad_down(kind, chip, half, side).wait_recv()
            gpart[kind, own_slot] = gpart[kind, own_slot] + ch_in[kind, chip].astype(F32)

        out[...] = gpart[kind, own_slot].astype(BF16)

    for d in range(1, look + 1):
        @pl.when(me - d >= 0)
        def _():
            seg_copy(d, side).wait_send()

    @pl.when(has_low)
    def _():
        down(kbuf, k_down, k_recv).wait_send()
        down(vbuf, v_down, v_recv).wait_send()

    @pl.when(not_top)
    def _():
        for kind in range(2):
            grad_up(kind).wait_send()

    @pl.loop(0, chip + end)
    def _(w):
        across(kbuf, k_side, k_recv, w).wait_send()
        across(vbuf, v_side, v_recv, w).wait_send()
        for kind in range(2):
            grad_side(kind, w).wait_send()

        @pl.when(jnp.logical_and(not_top, w <= chip))
        def _():
            for half in range(HALVES):
                up(kbuf, k_up, k_low, w, half, side).wait_send()
                up(vbuf, v_up, v_low, w, half, side).wait_send()

        @pl.when(w < chip)
        def _():
            for kind in range(2):
                for half in range(HALVES):
                    grad_down(kind, w, half, side).wait_send()


def pass_on(a_ref, b_ref, c_ref, a_out, b_out, c_out):
    a_out[...] = a_ref[...]
    b_out[...] = b_ref[...]
    c_out[...] = c_ref[...]


def per_device(queries, keys, values, grad_out, saved_out, segment_ids, frame_flags):
    ranks = lax.axis_size("ctx")
    chips = ranks // CORES
    key_rows = keys.shape[1]
    query_rows, width = queries.shape[1:]
    cols = query_rows * (width // HD)
    look = (SEG_MOST + key_rows - 2) // key_rows
    assert look <= CORES and ranks % CORES == 0
    chunk = math.gcd(key_rows, 512)
    parts = key_rows // chunk
    keep = ranks * key_rows * cols * 4 <= KEEP_BYTES
    kept = ranks if keep else 1
    dma = pltpu.SemaphoreType.DMA
    block = (key_rows, HD)
    grads = (2, chips) + block
    vmem = pl.BlockSpec(memory_space=pltpu.VMEM)
    grad_queries, grad_keys, grad_values = pl.pallas_call(
        functools.partial(fused, ranks, look, chunk, keep),
        out_shape=(
            jax.ShapeDtypeStruct((query_rows, width), BF16),
            jax.ShapeDtypeStruct(block, BF16),
            jax.ShapeDtypeStruct(block, BF16),
        ),
        in_specs=[vmem] * 7,
        out_specs=(vmem,) * 3,
        scratch_shapes=[
            pltpu.VMEM((ranks,) + block, BF16),
            pltpu.VMEM((ranks,) + block, BF16),
            pltpu.VMEM((kept, key_rows, cols), F32) if keep else pltpu.VMEM((8, 128), F32),
            pltpu.VMEM((kept * parts, 1, cols), F32),
            pltpu.VMEM((HD, cols), BF16),
            pltpu.VMEM((cols, HD), BF16),
            pltpu.VMEM((HD, cols), BF16),
            pltpu.VMEM((cols, HD), BF16),
            pltpu.VMEM((1, cols), jnp.int32),
            pltpu.VMEM((1, cols), F32),
            pltpu.VMEM((1, cols), F32),
            pltpu.VMEM((1, cols), F32),
            pltpu.VMEM((1, cols), F32),
            pltpu.VMEM((HD, cols), F32),
            pltpu.VMEM((2, ranks) + block, F32),
            pltpu.VMEM(grads, BF16),
            pltpu.VMEM(grads, BF16),
            pltpu.VMEM(grads, BF16),
            pltpu.VMEM(grads, BF16),
            pltpu.VMEM((2,) + block, BF16),
            pltpu.VMEM((look, 1, key_rows), jnp.int32),
            dma((chips, HALVES)), dma((chips, HALVES)), dma((chips,)), dma((1,)), dma((ranks,)),
            dma((chips, HALVES)), dma((chips, HALVES)), dma((chips,)), dma((1,)), dma((ranks,)),
            dma((2, chips)), dma((2, chips)), dma((2, chips, HALVES)), dma((2, chips, HALVES)),
            dma((2,)), dma((2,)), dma((look,)), dma((look,)),
        ],
        compiler_params=pltpu.CompilerParams(
            collective_id=0, has_side_effects=True, vmem_limit_bytes=60 * 1024 * 1024
        ),
        cost_estimate=pl.CostEstimate(
            flops=12 * cols * ranks * key_rows * HD,
            bytes_accessed=8 * cols * HD,
            transcendentals=cols * ranks * key_rows,
        ),
    )(queries[0], keys[0], values[0], grad_out[0], saved_out[0], segment_ids, frame_flags)
    results = pl.pallas_call(
        pass_on,
        out_shape=tuple(jax.ShapeDtypeStruct(r.shape, r.dtype) for r in (grad_queries, grad_keys, grad_values)),
        in_specs=[vmem] * 3,
        out_specs=(vmem,) * 3,
    )(grad_queries, grad_keys, grad_values)
    return tuple(r[None] for r in results)


def solution(mesh):
    return jax.shard_map(
        per_device,
        mesh=mesh,
        in_specs=(
            P("dp", "ctx", None),
            P("dp", "ctx", None),
            P("dp", "ctx", None),
            P("dp", "ctx", None),
            P("dp", "ctx", None),
            P("dp", "ctx"),
            P("dp", None),
        ),
        out_specs=(P("dp", "ctx", None), P("dp", "ctx", None), P("dp", "ctx", None)),
        check_vma=False,
    )
```

```python
import functools
import math

import jax
import jax.numpy as jnp
from jax import lax
from jax.experimental import pallas as pl
from jax.experimental.pallas import tpu as pltpu
from jax.sharding import PartitionSpec as P

HD = 128
SEG_MOST = 1024
CORES = 2
HALVES = 2
LOW = -1e30
FLOOR = -1e29
KEEP_BYTES = 20 * 1024 * 1024
F32 = jnp.float32
BF16 = jnp.bfloat16


def push(src, dst, send, recv, rank):
    return pltpu.make_async_remote_copy(
        src_ref=src,
        dst_ref=dst,
        send_sem=send,
        recv_sem=recv,
        device_id={"ctx": rank},
        device_id_type=pl.DeviceIdType.MESH,
    )


def fused(
    ranks, look, chunk, keep,
    q_ref, k_ref, v_ref, do_ref, o_ref, seg_ref, flag_ref,
    dq_ref, dk_ref, dv_ref,
    kbuf, vbuf, ebuf, tops, qcols, qrows, docols, dorows, reach, odot, top, total, lse, dqt,
    gpart, sib_out, sib_in, ch_out, ch_in, low_in, segs,
    k_up, k_low, k_side, k_down, k_recv, v_up, v_low, v_side, v_down, v_recv,
    gs_send, gs_recv, gc_send, gc_recv, gl_send, gl_recv, seg_send, seg_recv,
):
    chips = ranks // CORES
    key_rows = k_ref.shape[0]
    query_rows = q_ref.shape[0]
    heads = q_ref.shape[1] // HD
    cols = query_rows * heads
    parts = key_rows // chunk
    scale = 1.0 / math.sqrt(HD)
    factor = scale * math.log2(math.e)
    me = lax.axis_index("ctx")
    chip = me // CORES
    core = me % CORES
    side = chip * CORES + (1 - core)
    is_top = chip == chips - 1
    not_top = chip < chips - 1
    has_low = chip > 0
    own_slot = me
    reach_ranks = max(look, CORES)

    barrier = pltpu.get_barrier_semaphore()
    there = jnp.int32(0)
    for d in range(1, reach_ranks + 1):
        @pl.when(me + d < ranks)
        def _():
            pl.semaphore_signal(barrier, inc=1, device_id={"ctx": me + d},
                                device_id_type=pl.DeviceIdType.MESH)

        @pl.when(me - d >= 0)
        def _():
            pl.semaphore_signal(barrier, inc=1, device_id={"ctx": me - d},
                                device_id_type=pl.DeviceIdType.MESH)

        there = there + jnp.where(me + d < ranks, 1, 0) + jnp.where(me - d >= 0, 1, 0)
    kbuf[own_slot] = k_ref[...]
    vbuf[own_slot] = v_ref[...]
    pl.semaphore_wait(barrier, there)

    def up(buf, sems, recv, w, half, rank):
        rows = pl.ds(half * (key_rows // HALVES), key_rows // HALVES)
        place = buf.at[w * CORES + core, rows]
        return push(place, place, sems.at[w, half], recv.at[w, half], rank)

    def start_up(buf, sems, recv, w):
        for half in range(HALVES):
            up(buf, sems, recv, w, half, me + CORES).start()

    def from_below(buf, sems, recv, w, forward):
        for half in range(HALVES):
            up(buf, sems, recv, w, half, side).wait_recv()
            if forward:
                up(buf, sems, recv, w, half, me + CORES).start()

    def across(buf, sems, recv, w):
        slot = w * CORES + core
        return push(buf.at[slot], buf.at[slot], sems.at[w], recv.at[slot], side)

    def down(buf, sems, recv):
        return push(buf.at[own_slot], buf.at[own_slot], sems.at[0], recv.at[own_slot], me - CORES)

    def arrived(buf, sems, recv, slot):
        push(buf.at[slot], buf.at[slot], sems.at[0], recv.at[slot], side).wait_recv()

    def seg_copy(d, rank):
        return push(seg_ref, segs.at[d - 1], seg_send.at[d - 1], seg_recv.at[d - 1], rank)

    def grad_side(kind, w):
        return push(sib_out.at[kind, w], sib_in.at[kind, w], gs_send.at[kind, w], gs_recv.at[kind, w], side)

    def half_of(half):
        return pl.ds(half * (key_rows // HALVES), key_rows // HALVES)

    def grad_down(kind, w, half, rank):
        rows = half_of(half)
        return push(ch_out.at[kind, w, rows], ch_in.at[kind, w, rows],
                    gc_send.at[kind, w, half], gc_recv.at[kind, w, half], rank)

    def grad_up(kind):
        return push(ch_out.at[kind, chip + 1], low_in.at[kind], gl_send.at[kind], gl_recv.at[kind], me + CORES)

    @pl.when(not_top)
    def _():
        start_up(kbuf, k_up, k_low, chip)

    across(kbuf, k_side, k_recv, chip).start()
    for d in range(1, look + 1):
        @pl.when(me - d >= 0)
        def _():
            seg_copy(d, me - d).start()

    @pl.when(has_low)
    def _():
        down(kbuf, k_down, k_recv).start()
        down(vbuf, v_down, v_recv).start()

    across(vbuf, v_side, v_recv, chip).start()

    for h in range(heads):
        at = slice(h * HD, (h + 1) * HD)
        rows = slice(h * query_rows, (h + 1) * query_rows)
        q_h = q_ref[:, at]
        do_h = do_ref[:, at]
        qrows[rows, :] = q_h
        dorows[rows, :] = do_h
        qcols[:, rows] = q_h.T
        docols[:, rows] = do_h.T
        odot[:, rows] = jnp.sum((do_h.astype(F32) * o_ref[:, at].astype(F32)).T, axis=0, keepdims=True)
    top[...] = jnp.full(top.shape, FLOOR, F32)
    total[...] = jnp.zeros(total.shape, F32)
    dqt[...] = jnp.zeros(dqt.shape, F32)

    for d in range(1, look + 1):
        @pl.when(me + d < ranks)
        def _():
            seg_copy(d, side).wait_recv()

        @pl.when(me + d >= ranks)
        def _():
            segs[d - 1] = jnp.full(seg_ref.shape, 1 << 20, jnp.int32)

    seg_q = seg_ref[:, key_rows - query_rows:].astype(F32)
    seg_col = jnp.broadcast_to(seg_q, (HD, query_rows)).T
    counts = jnp.zeros((query_rows, HD), F32)
    for d in range(look + 1):
        for j in range(key_rows // HD):
            at = slice(j * HD, (j + 1) * HD)
            piece = (seg_ref[:, at] if d == 0 else segs[d - 1, :, at]).astype(F32)
            counts = counts + jnp.where(piece <= seg_col, 1.0, 0.0)
    count = jnp.sum(counts, axis=1, keepdims=True)
    segments = flag_ref.shape[1]
    ids = lax.broadcasted_iota(jnp.int32, (query_rows, segments), 1).astype(F32)
    flags = jnp.broadcast_to(flag_ref[...].astype(F32), (query_rows, segments))
    framed = jnp.sum(jnp.where(ids == seg_col[:, :1], flags, 0.0), axis=1, keepdims=True)
    local = (key_rows - query_rows) + lax.broadcasted_iota(jnp.int32, (query_rows, 1), 0).astype(F32)
    last = jnp.where(framed == 1.0, count - 1.0, local)
    last_row = jnp.broadcast_to(last, (query_rows, HD)).T[:1, :].astype(jnp.int32) + me * key_rows
    for h in range(heads):
        reach[:, h * query_rows:(h + 1) * query_rows] = last_row

    def rows_of(part):
        return pl.ds(pl.multiple_of(part * chunk, chunk), chunk)

    def scores_of(slot, part, masked):
        s = jnp.dot(kbuf[slot, rows_of(part), :], qcols[...], preferred_element_type=F32) * factor
        if masked:
            first = slot * key_rows + part * chunk
            pos = first + lax.broadcasted_iota(jnp.int32, (chunk, cols), 0)
            s = jnp.where(pos <= reach[...], s, LOW)
        return s

    def stats(slot, masked):
        @pl.loop(0, parts)
        def _(part):
            s = scores_of(slot, part, masked)
            here = jnp.maximum(jnp.max(s, axis=0, keepdims=True), FLOOR)
            e = jnp.exp2(s - here)
            if keep:
                ebuf[slot, rows_of(part), :] = e
                tops[slot * parts + part] = here
            old = top[...]
            new = jnp.maximum(old, here)
            total[...] = total[...] * jnp.exp2(old - new) + (
                jnp.sum(e, axis=0, keepdims=True) * jnp.exp2(here - new))
            top[...] = new

    def chip_stats(w, masked):
        @pl.loop(0, CORES)
        def _(b):
            slot = w * CORES + (core + b) % CORES

            @pl.when(b == 1)
            def _():
                arrived(kbuf, k_side, k_recv, slot)

            stats(slot, masked)

    def probs_of(slot, part, masked):
        if keep:
            return ebuf[slot, rows_of(part), :] * jnp.exp2(tops[slot * parts + part] - lse[...])
        return jnp.exp2(scores_of(slot, part, masked) - lse[...])

    def send_side(kind, w):
        sib_out[kind, w] = gpart[kind, w * CORES + (1 - core)].astype(BF16)
        grad_side(kind, w).start()

    def value_grads(w, masked):
        @pl.loop(0, CORES * parts)
        def _(i):
            slot = w * CORES + i // parts
            part = i % parts
            p = probs_of(slot, part, masked).astype(BF16)
            gpart[0, slot, rows_of(part), :] = jnp.dot(p, dorows[...], preferred_element_type=F32)

        send_side(0, w)

    def key_grads(w, masked):
        @pl.loop(0, CORES)
        def _(b):
            slot = w * CORES + (core + b) % CORES

            @pl.when(b == 1)
            def _():
                arrived(vbuf, v_side, v_recv, slot)

            @pl.loop(0, parts)
            def _(part):
                p = probs_of(slot, part, masked)
                dp = jnp.dot(vbuf[slot, rows_of(part), :], docols[...], preferred_element_type=F32)
                ds = (p * (dp - odot[...])).astype(BF16)
                gpart[1, slot, rows_of(part), :] = scale * jnp.dot(ds, qrows[...], preferred_element_type=F32)
                dqt[...] += jnp.dot(kbuf[slot, rows_of(part), :].T, ds, preferred_element_type=F32)

        send_side(1, w)

    def summed(kind, w):
        grad_side(kind, w).wait_recv()
        return gpart[kind, w * CORES + core] + sib_in[kind, w].astype(F32)

    def hand_down(kind, w):
        mine = gpart.at[kind, w * CORES + core]
        mine[...] = summed(kind, w)
        for half in range(HALVES):
            rows = half_of(half)

            @pl.when(not_top)
            def _():
                grad_down(kind, w, half, side).wait_recv()
                mine[rows, :] += ch_in[kind, w, rows, :].astype(F32)

            ch_out[kind, w, rows, :] = mine[rows, :].astype(BF16)
            grad_down(kind, w, half, me - CORES).start()

    @pl.when(not_top)
    def _():
        @pl.loop(1, chip + 1)
        def _(s):
            from_below(kbuf, k_up, k_low, chip - s, True)
            across(kbuf, k_side, k_recv, chip - s).start()

        start_up(vbuf, v_up, v_low, chip)

    chip_stats(chip, True)

    @pl.loop(1, chip + 1)
    def _(s):
        w = chip - s

        @pl.when(is_top)
        def _():
            from_below(kbuf, k_up, k_low, w, False)
            across(kbuf, k_side, k_recv, w).start()

        chip_stats(w, False)

    @pl.when(not_top)
    def _():
        arrived(kbuf, k_side, k_recv, (chip + 1) * CORES + core)
        across(kbuf, k_side, k_recv, chip + 1).start()
        chip_stats(chip + 1, True)

    lse[...] = top[...] + jnp.log(total[...]) * math.log2(math.e)

    @pl.loop(0, chip)
    def _(t):
        w = chip - 1 - t
        value_grads(w, False)

        @pl.when(not_top)
        def _():
            from_below(vbuf, v_up, v_low, w, True)
            across(vbuf, v_side, v_recv, w).start()

        @pl.when(jnp.logical_and(is_top, t > 0))
        def _():
            hand_down(0, w + 1)

    @pl.when(jnp.logical_and(is_top, has_low))
    def _():
        hand_down(0, 0)

    @pl.loop(0, chip)
    def _(t):
        w = t

        @pl.when(is_top)
        def _():
            from_below(vbuf, v_up, v_low, w, False)
            across(vbuf, v_side, v_recv, w).start()

        key_grads(w, False)

        hand_down(jnp.where(is_top, 1, 0), jnp.where(is_top, w, chip - 1 - t))

    end = jnp.where(not_top, 2, 1)

    @pl.loop(0, end)
    def _(t):
        w = chip + end - 1 - t

        @pl.when(jnp.logical_and(not_top, w == chip))
        def _():
            @pl.loop(0, chip)
            def _(s):
                hand_down(1, s)

        value_grads(w, True)

        @pl.when(w > chip)
        def _():
            arrived(vbuf, v_side, v_recv, w * CORES + core)
            across(vbuf, v_side, v_recv, w).start()

        key_grads(w, True)

        @pl.when(w > chip)
        def _():
            for kind in range(2):
                ch_out[kind, w] = summed(kind, w).astype(BF16)
                grad_up(kind).start()

    for h in range(heads):
        rows = slice(h * query_rows, (h + 1) * query_rows)
        dq_ref[:, h * HD:(h + 1) * HD] = (dqt[:, rows].T * scale).astype(BF16)

    for kind, out in ((0, dv_ref), (1, dk_ref)):
        gpart[kind, own_slot] = summed(kind, chip)

        @pl.when(has_low)
        def _():
            push(low_in.at[kind], low_in.at[kind], gl_send.at[kind], gl_recv.at[kind], side).wait_recv()
            gpart[kind, own_slot] = gpart[kind, own_slot] + low_in[kind].astype(F32)

        @pl.when(not_top)
        def _():
            for half in range(HALVES):
                grad_down(kind, chip, half, side).wait_recv()
            gpart[kind, own_slot] = gpart[kind, own_slot] + ch_in[kind, chip].astype(F32)

        out[...] = gpart[kind, own_slot].astype(BF16)

    for d in range(1, look + 1):
        @pl.when(me - d >= 0)
        def _():
            seg_copy(d, side).wait_send()

    @pl.when(has_low)
    def _():
        down(kbuf, k_down, k_recv).wait_send()
        down(vbuf, v_down, v_recv).wait_send()

    @pl.when(not_top)
    def _():
        for kind in range(2):
            grad_up(kind).wait_send()

    @pl.loop(0, chip + end)
    def _(w):
        across(kbuf, k_side, k_recv, w).wait_send()
        across(vbuf, v_side, v_recv, w).wait_send()
        for kind in range(2):
            grad_side(kind, w).wait_send()

        @pl.when(jnp.logical_and(not_top, w <= chip))
        def _():
            for half in range(HALVES):
                up(kbuf, k_up, k_low, w, half, side).wait_send()
                up(vbuf, v_up, v_low, w, half, side).wait_send()

        @pl.when(w < chip)
        def _():
            for kind in range(2):
                for half in range(HALVES):
                    grad_down(kind, w, half, side).wait_send()


def pass_on(a_ref, b_ref, c_ref, a_out, b_out, c_out):
    a_out[...] = a_ref[...]
    b_out[...] = b_ref[...]
    c_out[...] = c_ref[...]


def per_device(queries, keys, values, grad_out, saved_out, segment_ids, frame_flags):
    ranks = lax.axis_size("ctx")
    chips = ranks // CORES
    key_rows = keys.shape[1]
    query_rows, width = queries.shape[1:]
    cols = query_rows * (width // HD)
    look = (SEG_MOST + key_rows - 2) // key_rows
    assert look <= CORES and ranks % CORES == 0
    chunk = math.gcd(key_rows, 512)
    parts = key_rows // chunk
    keep = ranks * key_rows * cols * 4 <= KEEP_BYTES
    kept = ranks if keep else 1
    dma = pltpu.SemaphoreType.DMA
    block = (key_rows, HD)
    grads = (2, chips) + block
    vmem = pl.BlockSpec(memory_space=pltpu.VMEM)
    grad_queries, grad_keys, grad_values = pl.pallas_call(
        functools.partial(fused, ranks, look, chunk, keep),
        out_shape=(
            jax.ShapeDtypeStruct((query_rows, width), BF16),
            jax.ShapeDtypeStruct(block, BF16),
            jax.ShapeDtypeStruct(block, BF16),
        ),
        in_specs=[vmem] * 7,
        out_specs=(vmem,) * 3,
        scratch_shapes=[
            pltpu.VMEM((ranks,) + block, BF16),
            pltpu.VMEM((ranks,) + block, BF16),
            pltpu.VMEM((kept, key_rows, cols), F32) if keep else pltpu.VMEM((8, 128), F32),
            pltpu.VMEM((kept * parts, 1, cols), F32),
            pltpu.VMEM((HD, cols), BF16),
            pltpu.VMEM((cols, HD), BF16),
            pltpu.VMEM((HD, cols), BF16),
            pltpu.VMEM((cols, HD), BF16),
            pltpu.VMEM((1, cols), jnp.int32),
            pltpu.VMEM((1, cols), F32),
            pltpu.VMEM((1, cols), F32),
            pltpu.VMEM((1, cols), F32),
            pltpu.VMEM((1, cols), F32),
            pltpu.VMEM((HD, cols), F32),
            pltpu.VMEM((2, ranks) + block, F32),
            pltpu.VMEM(grads, BF16),
            pltpu.VMEM(grads, BF16),
            pltpu.VMEM(grads, BF16),
            pltpu.VMEM(grads, BF16),
            pltpu.VMEM((2,) + block, BF16),
            pltpu.VMEM((look, 1, key_rows), jnp.int32),
            dma((chips, HALVES)), dma((chips, HALVES)), dma((chips,)), dma((1,)), dma((ranks,)),
            dma((chips, HALVES)), dma((chips, HALVES)), dma((chips,)), dma((1,)), dma((ranks,)),
            dma((2, chips)), dma((2, chips)), dma((2, chips, HALVES)), dma((2, chips, HALVES)),
            dma((2,)), dma((2,)), dma((look,)), dma((look,)),
        ],
        compiler_params=pltpu.CompilerParams(
            collective_id=0, has_side_effects=True, vmem_limit_bytes=60 * 1024 * 1024
        ),
        cost_estimate=pl.CostEstimate(
            flops=12 * cols * ranks * key_rows * HD,
            bytes_accessed=8 * cols * HD,
            transcendentals=cols * ranks * key_rows,
        ),
    )(queries[0], keys[0], values[0], grad_out[0], saved_out[0], segment_ids, frame_flags)
    results = pl.pallas_call(
        pass_on,
        out_shape=tuple(jax.ShapeDtypeStruct(r.shape, r.dtype) for r in (grad_queries, grad_keys, grad_values)),
        in_specs=[vmem] * 3,
        out_specs=(vmem,) * 3,
    )(grad_queries, grad_keys, grad_values)
    return tuple(r[None] for r in results)


def solution(mesh):
    return jax.shard_map(
        per_device,
        mesh=mesh,
        in_specs=(
            P("dp", "ctx", None),
            P("dp", "ctx", None),
            P("dp", "ctx", None),
            P("dp", "ctx", None),
            P("dp", "ctx", None),
            P("dp", "ctx"),
            P("dp", None),
        ),
        out_specs=(P("dp", "ctx", None), P("dp", "ctx", None), P("dp", "ctx", None)),
        check_vma=False,
    )
```
